512 devices in a mesh: fsdp: 8 (over x_lo, y), dp: 64 (over x_hi, z, core).
Axes of the slice: x: 4 (x_hi: 2, x_lo: 2; x = x_hi * 2 + x_lo), y: 4, z: 16, core: 2. Of those that a mesh axis runs over, the one named last changes fastest.
Arguments:
- values: bfloat16 [64, 1536, 2048], P('dp', 'fsdp'), may hold values from -6 to 6
- cotangent: bfloat16 [64, 1536, 2048], P('dp', 'fsdp'), may hold values from -6 to 6
- out_weight: bfloat16 [2048, 2048], P(('fsdp', 'dp')), may hold values from -0.125 to 0.125
- gate_weight: bfloat16 [256, 2048], P(None, 'fsdp'), may hold values from -0.375 to 0.375
- in_probe: bfloat16 [2048, 64], replicated, may hold values from -0.125 to 0.125
- out_probe: bfloat16 [2048, 64], replicated, may hold values from -0.125 to 0.125
- timesteps: int32 [64], P('dp'), may hold values from 0 to 999
- text_lengths: int32 [64], P('dp'), may hold values from 1 to 256
Outputs:
- mixed_out: bfloat16 [64, 1536, 2048], P('dp', 'fsdp')
- grad_values: bfloat16 [64, 1536, 2048], P('dp', 'fsdp')
- projected: float32 [64, 64, 64], P('dp', 'fsdp')
- gate_weight_grad: float32 [256, 2048], P(None, 'fsdp')
The draws below stay inside these ranges and needn't reach their ends.
All inputs are finite; a program needn't handle non-finite values.
Results may differ from the reference program's by a relative error of at most 0.0057.
Values may be sent and summed in bfloat16 or wider, within the bound.
A program may use at most 64 MiB of HBM per device.

```python
import jax
import jax.numpy as jnp
from jax import lax

DIN = 2048
DOUT = 2048
FREQ = 256
R = 64
TXT = 256
SEQ = 1536
EXAMPLES = 64


def touch_ends(result, stream_key, smallest, high):
    shape = result.shape
    spot = [jax.random.randint(jax.random.fold_in(stream_key, axis), (), 0, shape[axis]) for axis in range(len(shape))]
    result = result.at[tuple(spot)].set(smallest)
    longest = shape.index(max(shape))
    spot[longest] = (spot[longest] + 1) % shape[longest]
    return result.at[tuple(spot)].set(high)


def block_levels(key, dims, cuts, least, largest):
    factor_of, own = 1.0, jax.random.fold_in(key, 6)
    for position, parts in cuts:
        heights = jnp.exp(jax.random.uniform(jax.random.fold_in(own, position), (parts,), jnp.float32, least / len(cuts), largest / len(cuts)))
        factor_of = factor_of * jnp.repeat(heights, dims[position] // parts).reshape([-1 if axis == position else 1 for axis in range(len(dims))])
    return factor_of


def gaussian(key, extent, scale, bound, shards=(), kind=jnp.bfloat16):
    entries = scale * jax.random.normal(key, extent, jnp.float32)
    if shards:
        entries = entries * block_levels(key, extent, shards, -0.22, 0.18)
    return jnp.clip(entries, -bound, bound).astype(kind)


def setup_inputs(seed: int = 0) -> dict:
    arg_keys = jax.random.split(jax.random.key(seed), 9)
    values = gaussian(arg_keys[0], (EXAMPLES, SEQ, DIN), 1.0, 6.0, ((0, 64), (1, 8)))
    cotangent = gaussian(arg_keys[1], (EXAMPLES, SEQ, DOUT), 1.0, 6.0, ((0, 64), (1, 8)))
    out_weight = gaussian(arg_keys[2], (DIN, DOUT), DIN ** -0.5, 0.125, ((0, 512),))
    gate_weight = gaussian(arg_keys[3], (FREQ, DOUT), FREQ ** -0.5, 0.375, ((1, 8),))
    in_probe = gaussian(arg_keys[4], (DIN, R), DIN ** -0.5, 0.125)
    out_probe = gaussian(arg_keys[5], (DOUT, R), DOUT ** -0.5, 0.125)
    timesteps = touch_ends(jax.random.randint(arg_keys[6], (EXAMPLES,), 0, 1000), jax.random.fold_in(arg_keys[6], 1), 0, 999).astype(jnp.int32)
    text_lengths = touch_ends(jax.random.randint(arg_keys[7], (EXAMPLES,), 1, TXT + 1), jax.random.fold_in(arg_keys[7], 1), 1, TXT).astype(jnp.int32)
    return {"values": values, "cotangent": cotangent, "out_weight": out_weight, "gate_weight": gate_weight, "in_probe": in_probe, "out_probe": out_probe, "timesteps": timesteps, "text_lengths": text_lengths}


def frequency_embedding(step_values, freq_width):
    half_width = freq_width // 2
    counter = jnp.arange(half_width, dtype=jnp.float32)
    frequencies = jnp.exp(-jnp.log(10000.0) * counter / half_width)
    angles = step_values.astype(jnp.float32)[:, None] * frequencies[None, :]
    return jnp.concatenate([jnp.cos(angles), jnp.sin(angles)], axis=-1)


def reference(values, cotangent, out_weight, gate_weight, in_probe, out_probe, timesteps, text_lengths):
    embedding = frequency_embedding(timesteps, FREQ)
    gate_scale = jnp.dot(embedding, gate_weight.astype(jnp.float32), precision=lax.Precision.HIGHEST)
    positions = jnp.arange(SEQ)
    valid_rows = (positions[None, :] < (SEQ - TXT) + text_lengths[:, None]).astype(jnp.float32)
    weight_turned = out_weight.T

    def per_example(items):
        inputs_row, grads_row, gate_row, valid_row = items
        branch = jnp.dot(inputs_row, out_weight, preferred_element_type=jnp.float32)
        mixed_row = (gate_row[None, :] * branch).astype(jnp.bfloat16)
        scaled = valid_row[:, None] * grads_row.astype(jnp.float32)
        masked = (scaled * gate_row[None, :]).astype(jnp.bfloat16)
        grad_row = jnp.dot(masked, weight_turned, preferred_element_type=jnp.float32).astype(jnp.bfloat16)
        gate_grads = jnp.sum(scaled * branch, axis=0)
        probe_in = jnp.dot(inputs_row, in_probe, preferred_element_type=jnp.float32).astype(jnp.bfloat16)
        probe_out = jnp.dot(masked, out_probe, preferred_element_type=jnp.float32).astype(jnp.bfloat16)
        projected_row = jnp.dot(probe_in.T, probe_out, preferred_element_type=jnp.float32) * (SEQ ** -0.5)
        return mixed_row, grad_row, projected_row, gate_grads

    mixed_out, grad_values, projected, gate_grads = lax.map(per_example, (values, cotangent, gate_scale, valid_rows))
    gate_weight_grad = jnp.dot(embedding.T, gate_grads, precision=lax.Precision.HIGHEST) * ((SEQ * EXAMPLES) ** -0.5)
    return mixed_out, grad_values, projected, gate_weight_grad
```

```python
import jax
import jax.numpy as jnp
from jax import lax
from jax.experimental import pallas as pl
from jax.experimental.pallas import tpu as pltpu
from jax.sharding import PartitionSpec as P

MESH = pl.DeviceIdType.MESH
F32, BF16 = jnp.float32, jnp.bfloat16
TXT = 256
H = 2
STEP = {0: -1, -1: 2}

AXIS = [(-1, 0), (0, -1), (1, 0), (0, 1), (2, 0), (0, 2)]
FORWARDED = [(i, -1, "A") for i in (-1, 1, 2)] + [(-1, j, "B") for j in (-1, 1, 2)]
FORWARDED = [FORWARDED[n] for n in (0, 3, 1, 4, 2, 5)]
FINAL = [(i, j, "A") for j in (1, 2) for i in (-1, 1, 2)] + [
    (i, j, "B") for i in (1, 2) for j in (-1, 1, 2)
]
FINAL = [FINAL[n] for n in (0, 6, 1, 7, 2, 8, 3, 9, 4, 10, 5, 11)]
MESSAGES = [(i, j, "AB") for i, j in AXIS] + FORWARDED + FINAL
INDEX = {message: n for n, message in enumerate(MESSAGES)}
OWN = len(MESSAGES)


def onward(message):
    i, j, part = message
    if part == "A":
        return [("yf", (i, 2, "A"))] if j == -1 else []
    if part == "B":
        return [("xf", (2, j, "B"))] if i == -1 else []
    if (i, j) == (0, 0):
        return [
            ("xf", (-1, 0, "AB")), ("yf", (0, -1, "AB")),
            ("xb", (1, 0, "AB")), ("yb", (0, 1, "AB")),
        ]
    if j == 0:
        first = [("xf", (2, 0, "AB"))] if i == -1 else []
        return first + [("yf", (i, -1, "A")), ("yb", (i, 1, "A"))]
    first = [("yf", (0, 2, "AB"))] if j == -1 else []
    return first + [("xf", (-1, j, "B")), ("xb", (1, j, "B"))]


def kernel(
    w_ref, emb_ref, len_ref, gw_ref, values_ref, cot_ref, inp_ref, outp_ref,
    mixed_out, grads_out, proj_out, gwg_out,
    wbuf, vals, cot, inp, outp, masked, mixed, grads, acc, gate,
    qbuf, psend, precv, eown, erecv, ebuf, tsend, trecv, town, t1recv, tbuf,
    l_sem, q_send, q_recv, g_send, g_recv, z_send, z_recv, x_send, x_recv, d_send, d_recv,
    p_send, p_recv, e1_send, e1_recv, e2_send, e2_recv, t0_send, t0_recv,
    t1_send, t1_recv, t2_send, t2_recv,
):
    f, d = lax.axis_index("fsdp"), lax.axis_index("dp")
    x_lo, y = f // 4, f % 4
    x_hi, z, c = d // 32, (d // 2) % 16, d % 2
    x = 2 * x_hi + x_lo
    s = 1 - 2 * c
    m, p = z // 2, z % 2

    def device(xx, yy, zz, cc):
        return ((xx % 2) * 4 + yy, (xx // 2) * 32 + zz * 2 + cc)

    def remote(src, dst, send, recv, target):
        return pltpu.make_async_remote_copy(
            src_ref=src, dst_ref=dst, send_sem=send, recv_sem=recv,
            device_id=target, device_id_type=MESH,
        )

    loads = [
        pltpu.make_async_copy(a, b, l_sem.at[n])
        for n, (a, b) in enumerate(
            ((values_ref, vals), (cot_ref, cot), (inp_ref, inp), (outp_ref, outp))
        )
    ]
    for load in loads:
        load.start()

    here = (f, d)
    core_peer = device(x, y, z, 1 - c)
    z_peers = [device(x, y, (z + k) % 16, c) for k in range(1, 16)]
    f_peers = [((f + k) % 8, d) for k in range(1, 8)]
    quad_peers = []
    for k in range(1, 4):
        t = (2 * x_hi + c + k) % 4
        quad_peers.append((f, (t // 2) * 32 + z * 2 + t % 2))
    way = {
        "xf": device((x + s + 4) % 4, y, z, c),
        "xb": device((x - s + 4) % 4, y, z, c),
        "yf": device(x, (y + s + 4) % 4, z, c),
        "yb": device(x, (y - s + 4) % 4, z, c),
    }

    barrier = pltpu.get_barrier_semaphore()
    greeted = z_peers + f_peers + quad_peers
    greeted = greeted + [
        (f, x_hi * 32 + (z + 1 - 2 * p) * 2 + 1 - c),
        ((1 - x_lo) * 4 + y, (1 - x_hi) * 32 + z * 2 + c),
    ]
    for peer in greeted:
        pl.semaphore_signal(barrier, inc=1, device_id=peer, device_id_type=MESH)

    mine = w_ref[...].astype(F32)
    t_own = 2 * p + c
    qbuf[t_own] = jnp.concatenate(
        [mine[:, 512 * n : 512 * n + 512] for n in range(4)], axis=0
    ).astype(BF16)
    pl.semaphore_wait(barrier, len(greeted))

    q_copies = []
    for k in range(1, 4):
        t = (t_own + k) % 4
        target = device(x, y, 2 * m + t // 2, t % 2)
        copy = remote(qbuf.at[t_own], qbuf.at[t_own], q_send.at[k], q_recv.at[k], target)
        copy.start()
        q_copies.append(copy)

    emb = emb_ref[...]
    share = jnp.dot(
        jnp.broadcast_to(emb, (8, 256)), gw_ref[...].astype(F32),
        precision=lax.Precision.HIGHEST, preferred_element_type=F32,
    )
    f_cols = pl.ds(pl.multiple_of(256 * f, 256), 256)
    gate[:, f_cols] = share
    g_copies = []
    for k in range(1, 8):
        copy = remote(gate.at[:, f_cols], gate.at[:, f_cols], g_send.at[k], g_recv.at[k], f_peers[k - 1])
        copy.start()
        g_copies.append(copy)

    for copy in q_copies:
        copy.wait_recv()
    quarter = [qbuf[t].astype(F32) for t in range(4)]
    low, high = [
        jnp.concatenate(
            [
                jnp.concatenate([quarter[t][4 * n : 4 * n + 4] for t in range(4)], axis=0)
                for n in pair
            ],
            axis=1,
        )
        for pair in ((0, 1), (2, 3))
    ]

    def row_of(i, j):
        xx, yy = (x + s * i + 8) % 4, (y + s * j + 8) % 4
        return (xx % 2) * 1024 + yy * 256 + (xx // 2) * 128

    def cols_of(core, h, part):
        start = 1024 * core + (1024 // H) * h + (512 // H if part == "B" else 0)
        width = 1024 // H if part == "AB" else 512 // H
        return pl.ds(pl.multiple_of(start, 128), width)

    own_rows = pl.ds(pl.multiple_of(row_of(0, 0) + 16 * m, 16), 16)
    half_cols = pl.ds(pl.multiple_of(1024 * c, 1024), 1024)
    wbuf[own_rows, half_cols] = jnp.where(c == 0, low, high).astype(BF16)

    sent = []
    z_copies = {}
    for h in range(H):
        cols = cols_of(c, h, "AB")
        block = wbuf.at[own_rows, cols]
        for k in range(1, 8):
            to = (z + (2 * p - 1) * k + 16) % 16
            away = (to // 2 - m + 8) % 8
            copy = remote(block, block, z_send.at[h, k], z_recv.at[h, away], device(x, y, to, c))
            copy.start()
            sent.append(copy)

    def z_wait(h):
        block = wbuf.at[own_rows, cols_of(c, h, "AB")]
        for away in range(1, 8):
            remote(block, block, z_send.at[h, away], z_recv.at[h, away], core_peer).wait_recv()

    def block_of(core, h, message):
        i, j, part = message
        rows = pl.ds(pl.multiple_of(row_of(i, j), 128), 128)
        return wbuf.at[rows, cols_of(core, h, part)]


    def part_block(h, message, part):
        return block_of(c, h, (message[0], message[1], part))

    def forward(h, message):
        i, j, part = message
        for direction, there in onward(message):
            n = INDEX[there]
            block = part_block(h, message, there[2])
            copy = remote(block, block, x_send.at[h, n], x_recv.at[h, n], way[direction])
            copy.start()
            sent.append(copy)
        n = OWN if (i, j) == (0, 0) else INDEX[message]
        block = block_of(c, h, message)
        copy = remote(block, block, d_send.at[h, n], d_recv.at[h, n], core_peer)
        copy.start()
        sent.append(copy)

    def take(h, message):
        n = INDEX[message]
        block = block_of(c, h, message)
        remote(block, block, x_send.at[h, n], x_recv.at[h, n], core_peer).wait_recv()
        forward(h, message)

    def other_core(h):
        for n, message in enumerate(MESSAGES + [(0, 0, "AB")]):
            block = block_of(1 - c, h, message)
            remote(block, block, d_send.at[h, n], d_recv.at[h, n], core_peer).wait_recv()

    e = 2 * x_hi + c
    tile_row = lax.broadcasted_iota(jnp.int32, (8, 128), 0)

    def tile_of(row):
        low = jnp.broadcast_to(row[:, :128], (8, 128))
        high = jnp.broadcast_to(row[:, 128:], (8, 128))
        zero = jnp.zeros((8, 128), F32)
        return jnp.where(tile_row == e, low, jnp.where(tile_row == e + 4, high, zero))

    eown[...] = tile_of(emb)
    e_copies = []
    for k in range(1, 4):
        copy = remote(eown, erecv.at[k], e1_send.at[k], e1_recv.at[k], quad_peers[k - 1])
        copy.start()
        e_copies.append(copy)

    z_wait(0)
    forward(0, (0, 0, "AB"))

    for copy in g_copies:
        copy.wait_recv()
    for load in loads:
        load.wait()
    limit = 8 * 192 - TXT + len_ref[0]

    def valid(width):
        return lax.broadcasted_iota(jnp.int32, (192, width), 0) + f * 192 < limit

    @pl.loop(0, 8)
    def _(n):
        cols = pl.ds(pl.multiple_of(n * 256, 256), 256)
        scaled = jnp.where(valid(256), cot[:, cols].astype(F32), 0.0)
        masked[:, cols] = (scaled * gate[0:1, cols]).astype(BF16)

    for i, j in AXIS:
        take(0, (i, j, "AB"))
    z_wait(1)
    forward(1, (0, 0, "AB"))
    for message in FORWARDED:
        take(0, message)

    for copy in e_copies:
        copy.wait_recv()
    ebuf[z] = eown[...] + erecv[1] + erecv[2] + erecv[3]
    e2_copies = []
    for k in range(1, 16):
        copy = remote(ebuf.at[z], ebuf.at[z], e2_send.at[k], e2_recv.at[k], z_peers[k - 1])
        copy.start()
        e2_copies.append(copy)

    for i, j in AXIS:
        take(1, (i, j, "AB"))

    probe_in = jnp.dot(vals[...], inp[...], preferred_element_type=F32).astype(BF16)
    probe_out = jnp.dot(masked[...], outp[...], preferred_element_type=F32).astype(BF16)
    projected = lax.dot_general(
        probe_in, probe_out, (((0,), (0,)), ((), ())), preferred_element_type=F32
    ) * (8 * 192) ** (-0.5)
    psend[...] = projected.reshape(8, 8, 64)
    p_copies = []
    for k in range(1, 8):
        copy = remote(psend.at[(f + k) % 8], precv.at[k], p_send.at[k], p_recv.at[k], f_peers[k - 1])
        copy.start()
        p_copies.append(copy)

    for message in FINAL:
        take(0, message)
    for message in FORWARDED:
        take(1, message)

    def branch(start):
        cols = pl.ds(pl.multiple_of(start, 256), 256)
        product = jnp.dot(vals[...], wbuf[:, cols], preferred_element_type=F32)
        mixed[:, cols] = (product * gate[0:1, cols]).astype(BF16)
        scaled = jnp.where(valid(256), cot[:, cols].astype(F32), 0.0)
        tsend[start // 256] = tile_of(jnp.sum(scaled * product, axis=0, keepdims=True))

    def branches(h):
        @pl.loop(0, 4)
        def _(n):
            branch((n // 2) * 1024 + h * 512 + (n % 2) * 256)

    def grad(h, n):
        rows = pl.ds(pl.multiple_of(n * 256, 256), 256)
        total = 0.0 if h == 0 else acc[:, rows]
        for core in range(2):
            cols = slice(1024 * core + 512 * h, 1024 * core + 512 * h + 512)
            total = total + lax.dot_general(
                masked[:, cols], wbuf[rows, cols], (((1,), (1,)), ((), ())),
                preferred_element_type=F32,
            )
        if h == 0:
            acc[:, rows] = total
        else:
            grads[:, rows] = total.astype(BF16)

    other_core(0)
    branches(0)
    for n in range(0, 6):
        take(1, FINAL[n])
    pl.loop(0, 8)(lambda n: grad(0, n))
    for n in range(6, 12):
        take(1, FINAL[n])

    other_core(1)
    branches(1)
    store_mixed = pltpu.make_async_copy(mixed, mixed_out, l_sem.at[4])
    store_mixed.start()

    t0_copies = []
    for k in range(1, 8):
        copy = remote(tsend.at[(f + k) % 8], trecv.at[k], t0_send.at[k], t0_recv.at[k], f_peers[k - 1])
        copy.start()
        t0_copies.append(copy)
    pl.loop(0, 4)(lambda n: grad(1, n))
    total = tsend[f]
    for k in range(1, 8):
        t0_copies[k - 1].wait_recv()
        total = total + trecv[k]
    town[...] = total
    t1_copies = []
    for k in range(1, 4):
        copy = remote(town, t1recv.at[k], t1_send.at[k], t1_recv.at[k], quad_peers[k - 1])
        copy.start()
        t1_copies.append(copy)
    pl.loop(4, 8)(lambda n: grad(1, n))
    store_grads = pltpu.make_async_copy(grads, grads_out, l_sem.at[5])
    store_grads.start()
    for copy in t1_copies:
        copy.wait_recv()
    tbuf[z] = town[...] + t1recv[1] + t1recv[2] + t1recv[3]
    t2_copies = []
    for k in range(1, 16):
        copy = remote(tbuf.at[z], tbuf.at[z], t2_send.at[k], t2_recv.at[k], z_peers[k - 1])
        copy.start()
        t2_copies.append(copy)

    total = psend[f]
    for k in range(1, 8):
        p_copies[k - 1].wait_recv()
        total = total + precv[k]
    proj_out[...] = total
    for copy in q_copies + g_copies + sent + e_copies + e2_copies + p_copies + t0_copies + t1_copies:
        copy.wait_send()
    for copy in e2_copies:
        copy.wait_recv()
    for copy in t2_copies:
        copy.wait()

    emb_all = ebuf[...].reshape(128, 128)
    grad_all = tbuf[...].reshape(128, 128)
    in_high = lax.broadcasted_iota(jnp.int32, (128, 128), 0) % 8 >= 4
    for half in range(2):
        ours = jnp.where(in_high if half else jnp.logical_not(in_high), grad_all, 0.0)
        for k_half in range(2):
            rows = emb_all
            if k_half != half:
                rows = pltpu.roll(emb_all, 4 if half else 124, 0)
            gwg_out[128 * k_half : 128 * k_half + 128, 128 * half : 128 * half + 128] = (
                lax.dot_general(
                    rows, ours, (((0,), (0,)), ((), ())),
                    precision=lax.Precision.HIGHEST, preferred_element_type=F32,
                ) * (8 * 192 * 64) ** (-0.5)
            )
    store_mixed.wait()
    store_grads.wait()


def frequency_embedding(step_values, freq_width):
    half_width = freq_width // 2
    counter = jnp.arange(half_width, dtype=jnp.float32)
    frequencies = jnp.exp(-jnp.log(10000.0) * counter / half_width)
    angles = step_values.astype(jnp.float32)[:, None] * frequencies[None, :]
    return jnp.concatenate([jnp.cos(angles), jnp.sin(angles)], axis=-1)


def per_device(
    values, cotangent, out_weight, gate_weight, in_probe, out_probe, timesteps, text_lengths
):
    embedding = frequency_embedding(timesteps, 256)
    vmem = pl.BlockSpec(memory_space=pltpu.VMEM)
    smem = pl.BlockSpec(memory_space=pltpu.SMEM)
    anywhere = pl.BlockSpec(memory_space=pl.ANY)
    dma = pltpu.SemaphoreType.DMA
    count = OWN + 1
    mixed, grads, projected, gwg = pl.pallas_call(
        kernel,
        out_shape=(
            jax.ShapeDtypeStruct((192, 2048), BF16),
            jax.ShapeDtypeStruct((192, 2048), BF16),
            jax.ShapeDtypeStruct((8, 64), F32),
            jax.ShapeDtypeStruct((256, 256), F32),
        ),
        in_specs=[vmem, vmem, smem, vmem, anywhere, anywhere, anywhere, anywhere],
        out_specs=(anywhere, anywhere, vmem, vmem),
        scratch_shapes=[
            pltpu.VMEM((2048, 2048), BF16),
            pltpu.VMEM((192, 2048), BF16),
            pltpu.VMEM((192, 2048), BF16),
            pltpu.VMEM((2048, 64), BF16),
            pltpu.VMEM((2048, 64), BF16),
            pltpu.VMEM((192, 2048), BF16),
            pltpu.VMEM((192, 2048), BF16),
            pltpu.VMEM((192, 2048), BF16),
            pltpu.VMEM((192, 2048), F32),
            pltpu.VMEM((8, 2048), F32),
            pltpu.VMEM((4, 16, 512), BF16),
            pltpu.VMEM((8, 8, 64), F32),
            pltpu.VMEM((8, 8, 64), F32),
            pltpu.VMEM((8, 128), F32),
            pltpu.VMEM((4, 8, 128), F32),
            pltpu.VMEM((16, 8, 128), F32),
            pltpu.VMEM((8, 8, 128), F32),
            pltpu.VMEM((8, 8, 128), F32),
            pltpu.VMEM((8, 128), F32),
            pltpu.VMEM((4, 8, 128), F32),
            pltpu.VMEM((16, 8, 128), F32),
            dma((6,)),
            dma((4,)), dma((4,)),
            dma((8,)), dma((8,)),
            dma((H, 8)), dma((H, 8)),
            dma((H, count)), dma((H, count)),
            dma((H, count)), dma((H, count)),
            dma((8,)), dma((8,)),
            dma((4,)), dma((4,)),
            dma((16,)), dma((16,)),
            dma((8,)), dma((8,)),
            dma((4,)), dma((4,)),
            dma((16,)), dma((16,)),
        ],
        compiler_params=pltpu.CompilerParams(
            collective_id=0, has_side_effects=True, vmem_limit_bytes=40 * 1024 * 1024
        ),
        cost_estimate=pl.CostEstimate(
            flops=4 * 192 * 2048 * 2048, bytes_accessed=8 * 192 * 2048, transcendentals=0
        ),
    )(
        out_weight, embedding, text_lengths, gate_weight,
        values[0], cotangent[0], in_probe, out_probe,
    )
    return mixed[None], grads[None], projected[None], gwg


def solution(mesh):
    in_specs = (
        P("dp", "fsdp", None),
        P("dp", "fsdp", None),
        P(("fsdp", "dp"), None),
        P(None, "fsdp"),
        P(),
        P(),
        P("dp"),
        P("dp"),
    )
    out_specs = (
        P("dp", "fsdp", None),
        P("dp", "fsdp", None),
        P("dp", "fsdp", None),
        P(None, "fsdp"),
    )
    return jax.shard_map(
        per_device, mesh=mesh, in_specs=in_specs, out_specs=out_specs, check_vma=False
    )
```

```python
import jax
import jax.numpy as jnp
from jax import lax
from jax.experimental import pallas as pl
from jax.experimental.pallas import tpu as pltpu
from jax.sharding import PartitionSpec as P

MESH = pl.DeviceIdType.MESH
F32, BF16 = jnp.float32, jnp.bfloat16
TXT = 256
GROUPS = ((0, 48), (48, 80))
SLOTS = ((1, 2), (3, 4, 5, 6, 7))
H = len(GROUPS)

AXIS = [(-1, 0), (0, -1), (1, 0), (0, 1), (2, 0), (0, 2)]
FORWARDED = [(i, -1, "A") for i in (-1, 1, 2)] + [(-1, j, "B") for j in (-1, 1, 2)]
FORWARDED = [FORWARDED[n] for n in (0, 3, 1, 4, 2, 5)]
FINAL = [(i, j, "A") for j in (1, 2) for i in (-1, 1, 2)] + [
    (i, j, "B") for i in (1, 2) for j in (-1, 1, 2)
]
FINAL = [FINAL[n] for n in (0, 6, 1, 7, 2, 8, 3, 9, 4, 10, 5, 11)]
SIDE = [message for message in FINAL if message[:2] in ((-1, 1), (1, 1), (1, -1), (1, 2), (2, 1))]
SIDE = [message for message in SIDE if message not in ((1, 2, "A"), (2, 1, "B"))]
LAST = [message for message in FINAL if message not in SIDE]
MESSAGES = [(i, j, "AB") for i, j in AXIS] + FORWARDED + FINAL
INDEX = {message: n for n, message in enumerate(MESSAGES)}
OWN = len(MESSAGES)


def onward(message):
    i, j, part = message
    if part == "A":
        return [("yf", (i, 2, "A"))] if j == -1 else []
    if part == "B":
        return [("xf", (2, j, "B"))] if i == -1 else []
    if (i, j) == (0, 0):
        return [
            ("xf", (-1, 0, "AB")), ("yf", (0, -1, "AB")),
            ("xb", (1, 0, "AB")), ("yb", (0, 1, "AB")),
        ]
    if j == 0:
        first = [("xf", (2, 0, "AB"))] if i == -1 else []
        return first + [("yf", (i, -1, "A")), ("yb", (i, 1, "A"))]
    first = [("yf", (0, 2, "AB"))] if j == -1 else []
    return first + [("xf", (-1, j, "B")), ("xb", (1, j, "B"))]


def kernel(
    w_ref, emb_ref, len_ref, gw_ref, values_ref, cot_ref, inp_ref, outp_ref,
    mixed_out, grads_out, proj_out, gwg_out,
    wbuf, vals, cot, inp, outp, gw, valsp, place, masked, mixed, grads, acc, gate,
    qbuf, psend, precv, eown, erecv, ebuf, tsend, trecv, tbuf,
    l_sem, q_send, q_recv, g_send, g_recv, z_send, z_recv, x_send, x_recv, d_send, d_recv,
    p_send, p_recv, e1_send, e1_recv, e2_send, e2_recv, t1_send, t1_recv, t2_send, t2_recv,
):
    f, d = lax.axis_index("fsdp"), lax.axis_index("dp")
    x_lo, y = f // 4, f % 4
    x_hi, z, c = d // 32, (d // 2) % 16, d % 2
    x = 2 * x_hi + x_lo
    s = 1 - 2 * c
    m, p = z // 2, z % 2

    def device(xx, yy, zz, cc):
        return ((xx % 2) * 4 + yy, (xx // 2) * 32 + zz * 2 + cc)

    def remote(src, dst, send, recv, target):
        return pltpu.make_async_remote_copy(
            src_ref=src, dst_ref=dst, send_sem=send, recv_sem=recv,
            device_id=target, device_id_type=MESH,
        )

    loads = [
        pltpu.make_async_copy(a, b, l_sem.at[n])
        for n, (a, b) in enumerate(
            ((gw_ref, gw), (values_ref, vals), (cot_ref, cot), (inp_ref, inp), (outp_ref, outp))
        )
    ]
    for load in loads:
        load.start()

    here = (f, d)
    core_peer = device(x, y, z, 1 - c)
    z_peers = [device(x, y, (z + k) % 16, c) for k in range(1, 16)]
    f_peers = [((f + k) % 8, d) for k in range(1, 8)]
    quad_peers = []
    for k in range(1, 4):
        t = (2 * x_hi + c + k) % 4
        quad_peers.append((f, (t // 2) * 32 + z * 2 + t % 2))
    way = {
        "xf": device((x + s + 4) % 4, y, z, c),
        "xb": device((x - s + 4) % 4, y, z, c),
        "yf": device(x, (y + s + 4) % 4, z, c),
        "yb": device(x, (y - s + 4) % 4, z, c),
    }

    barrier = pltpu.get_barrier_semaphore()
    greeted = z_peers + f_peers + quad_peers
    greeted = greeted + [
        (f, x_hi * 32 + (z + 1 - 2 * p) * 2 + 1 - c),
        ((1 - x_lo) * 4 + y, (1 - x_hi) * 32 + z * 2 + c),
    ]
    for peer in greeted:
        pl.semaphore_signal(barrier, inc=1, device_id=peer, device_id_type=MESH)

    mine = w_ref[...].astype(F32)
    t_own = 2 * p + c
    qbuf[t_own] = jnp.concatenate(
        [mine[:, 512 * n : 512 * n + 512] for n in range(4)], axis=0
    ).astype(BF16)
    pl.semaphore_wait(barrier, len(greeted))

    q_copies = []
    for k in range(1, 4):
        t = (t_own + k) % 4
        target = device(x, y, 2 * m + t // 2, t % 2)
        copy = remote(qbuf.at[t_own], qbuf.at[t_own], q_send.at[k], q_recv.at[k], target)
        copy.start()
        q_copies.append(copy)

    emb = emb_ref[...]
    loads[0].wait()
    share = jnp.dot(
        jnp.broadcast_to(emb, (8, 256)), gw[...].astype(F32),
        precision=lax.Precision.HIGHEST, preferred_element_type=F32,
    )
    f_cols = pl.ds(pl.multiple_of(256 * f, 256), 256)
    gate[:, f_cols] = share
    g_copies = []
    for k in range(1, 8):
        copy = remote(gate.at[:, f_cols], gate.at[:, f_cols], g_send.at[k], g_recv.at[k], f_peers[k - 1])
        copy.start()
        g_copies.append(copy)

    for copy in q_copies:
        copy.wait_recv()
    quarter = [qbuf[t].astype(F32) for t in range(4)]
    low, high = [
        jnp.concatenate(
            [
                jnp.concatenate([quarter[t][4 * n : 4 * n + 4] for t in range(4)], axis=0)
                for n in pair
            ],
            axis=1,
        )
        for pair in ((0, 1), (2, 3))
    ]

    def row_of(i, j):
        xx, yy = (x + s * i + 8) % 4, (y + s * j + 8) % 4
        return (xx % 2) * 1024 + yy * 256 + (xx // 2) * 128

    def cols_of(core, part):
        start = 1024 * core + (512 if part == "B" else 0)
        return pl.ds(pl.multiple_of(start, 512), 1024 if part == "AB" else 512)

    own = row_of(0, 0)
    own_rows = pl.ds(pl.multiple_of(own, 16), 16)
    half_cols = cols_of(c, "AB")
    wbuf[own_rows, half_cols] = jnp.where(c == 0, low, high).astype(BF16)

    sent = []
    for k in range(1, 8):
        away = (k + 1) // 2
        slot = 2 * away - 1 + (p if away < 4 else 0)
        there = pl.ds(pl.multiple_of(own + 16 * slot, 16), 16)
        copy = remote(
            wbuf.at[own_rows, half_cols], wbuf.at[there, half_cols], z_send.at[k], z_recv.at[slot],
            device(x, y, (z + (2 * p - 1) * k + 16) % 16, c),
        )
        copy.start()
        sent.append(copy)

    def z_wait(h):
        for slot in SLOTS[h]:
            block = wbuf.at[pl.ds(pl.multiple_of(own + 16 * slot, 16), 16), half_cols]
            remote(block, block, z_send.at[slot], z_recv.at[slot], core_peer).wait_recv()

    def block_of(core, h, message):
        i, j, part = message
        first, count = GROUPS[h]
        rows = pl.ds(pl.multiple_of(row_of(i, j) + first, 16), count)
        return wbuf.at[rows, cols_of(core, part)]


    def part_block(h, message, part):
        return block_of(c, h, (message[0], message[1], part))

    def forward(h, message):
        i, j, part = message
        for direction, there in onward(message):
            n = INDEX[there]
            block = part_block(h, message, there[2])
            copy = remote(block, block, x_send.at[h, n], x_recv.at[h, n], way[direction])
            copy.start()
            sent.append(copy)
        n = OWN if (i, j) == (0, 0) else INDEX[message]
        block = block_of(c, h, message)
        copy = remote(block, block, d_send.at[h, n], d_recv.at[h, n], core_peer)
        copy.start()
        sent.append(copy)

    def take(h, message):
        n = INDEX[message]
        block = block_of(c, h, message)
        remote(block, block, x_send.at[h, n], x_recv.at[h, n], core_peer).wait_recv()
        forward(h, message)

    def from_other_core(i, j):
        i_there, j_there = (-i if i % 2 else i), (-j if j % 2 else j)
        for h in range(H):
            for part in ("AB",) if 0 in (i, j) else ("A", "B"):
                n = OWN if (i, j) == (0, 0) else INDEX[(i_there, j_there, part)]
                block = block_of(1 - c, h, (i, j, part))
                remote(block, block, d_send.at[h, n], d_recv.at[h, n], core_peer).wait_recv()

    e = 2 * x_hi + c
    tile_row = lax.broadcasted_iota(jnp.int32, (8, 128), 0)

    def tile_of(row):
        low = jnp.broadcast_to(row[:, :128], (8, 128))
        high = jnp.broadcast_to(row[:, 128:], (8, 128))
        zero = jnp.zeros((8, 128), F32)
        return jnp.where(tile_row == e, low, jnp.where(tile_row == e + 4, high, zero))

    eown[...] = tile_of(emb)
    e_copies = []
    for k in range(1, 4):
        copy = remote(eown, erecv.at[k], e1_send.at[k], e1_recv.at[k], quad_peers[k - 1])
        copy.start()
        e_copies.append(copy)

    z_wait(0)
    forward(0, (0, 0, "AB"))

    for copy in g_copies:
        copy.wait_recv()
    for load in loads[1:]:
        load.wait()
    limit = 8 * 192 - TXT + len_ref[0]

    def valid(width):
        return lax.broadcasted_iota(jnp.int32, (192, width), 0) + f * 192 < limit

    @pl.loop(0, 8)
    def _(n):
        cols = pl.ds(pl.multiple_of(n * 256, 256), 256)
        scaled = jnp.where(valid(256), cot[:, cols].astype(F32), 0.0)
        masked[:, cols] = (scaled * gate[0:1, cols]).astype(BF16)

    k_at = lax.broadcasted_iota(jnp.int32, (128, 128), 0)
    n_at = lax.broadcasted_iota(jnp.int32, (128, 128), 1)
    slot_at = n_at // 16
    away_at = jnp.where(slot_at % 2 == 1, (slot_at + 1) // 2, 8 - slot_at // 2)
    place[...] = jnp.where(k_at == (m + away_at) % 8 * 16 + n_at % 16, 1.0, 0.0).astype(BF16)

    @pl.loop(0, 16)
    def _(n):
        cols = pl.ds(pl.multiple_of(n * 128, 128), 128)
        valsp[:, cols] = jnp.dot(
            vals[:, cols], place[...], preferred_element_type=F32
        ).astype(BF16)

    for i, j in AXIS:
        take(0, (i, j, "AB"))
    z_wait(1)
    forward(1, (0, 0, "AB"))
    for message in FORWARDED:
        take(0, message)

    for copy in e_copies:
        copy.wait_recv()
    ebuf[z] = eown[...] + erecv[1] + erecv[2] + erecv[3]
    e2_copies = []
    for k in range(1, 16):
        copy = remote(ebuf.at[z], ebuf.at[z], e2_send.at[k], e2_recv.at[k], z_peers[k - 1])
        copy.start()
        e2_copies.append(copy)

    for i, j in AXIS:
        take(1, (i, j, "AB"))

    turned = (((1,), (1,)), ((), ()))
    probe_in = lax.dot_general(vals[...], inp[...], turned, preferred_element_type=F32).astype(BF16)
    probe_out = lax.dot_general(masked[...], outp[...], turned, preferred_element_type=F32).astype(BF16)
    projected = lax.dot_general(
        probe_in, probe_out, (((0,), (0,)), ((), ())), preferred_element_type=F32
    ) * (8 * 192) ** (-0.5)
    psend[...] = projected.reshape(8, 8, 64)
    p_copies = []
    for k in range(1, 8):
        copy = remote(psend.at[(f + k) % 8], precv.at[k], p_send.at[k], p_recv.at[k], f_peers[k - 1])
        copy.start()
        p_copies.append(copy)

    for message in FINAL:
        take(0, message)

    def pair_rows(i, j):
        xx, yy = (x + i + 8) % 2, (y + s * j + 8) % 4
        return pl.ds(pl.multiple_of(xx * 1024 + yy * 256, 256), 256)

    def branch(i, j, first=False):
        rows = pair_rows(i, j)

        @pl.loop(0, 8)
        def _(n):
            cols = pl.ds(pl.multiple_of(n * 256, 256), 256)
            product = jnp.dot(valsp[:, rows], wbuf[rows, cols], preferred_element_type=F32)
            acc[:, cols] = product if first else acc[:, cols] + product

    def grad(i, j):
        rows = pair_rows(i, j)
        slots = lax.dot_general(
            masked[...], wbuf[rows, :], turned, preferred_element_type=F32
        ).astype(BF16)
        for n in range(2):
            cols = pl.ds(pl.multiple_of(rows.start + 128 * n, 128), 128)
            grads[:, cols] = lax.dot_general(
                slots[:, 128 * n : 128 * n + 128], place[...], turned, preferred_element_type=F32
            ).astype(BF16)

    def pair_wait(i, j):
        for i_each in (0, 2) if i == 0 else (-1, 1):
            from_other_core(i_each, j)

    for message in FORWARDED:
        take(1, message)
    pair_wait(0, 0)
    branch(0, 0, first=True)
    pair_wait(1, 0)
    branch(1, 0)
    for message in SIDE:
        take(1, message)
    grad(0, 0)
    grad(1, 0)
    for j in (-1, 1):
        pair_wait(1, j)
        branch(1, j)
        grad(1, j)
    for message in LAST:
        take(1, message)
    for i, j in ((0, -1), (0, 1), (1, 2), (0, 2)):
        pair_wait(i, j)
        branch(i, j)

    @pl.loop(0, 8)
    def _(n):
        cols = pl.ds(pl.multiple_of(n * 256, 256), 256)
        product = acc[:, cols]
        scaled = jnp.where(valid(256), cot[:, cols].astype(F32), 0.0)
        tsend[n] = tile_of(jnp.sum(scaled * product, axis=0, keepdims=True))
        mixed[:, cols] = (product * gate[0:1, cols]).astype(BF16)

    t1_copies = []
    for k in range(8):
        to_f = (f + k) % 8
        for k_quad in range(4):
            n = 4 * k + k_quad
            if n:
                t = (e + k_quad) % 4
                target = (to_f, (t // 2) * 32 + z * 2 + t % 2)
                copy = remote(tsend.at[to_f], trecv.at[n], t1_send.at[n], t1_recv.at[n], target)
                copy.start()
                t1_copies.append(copy)
    store_mixed = pltpu.make_async_copy(mixed, mixed_out, l_sem.at[5])
    store_mixed.start()
    for i, j in ((0, -1), (0, 1), (1, 2), (0, 2)):
        grad(i, j)
    store_grads = pltpu.make_async_copy(grads, grads_out, l_sem.at[6])
    store_grads.start()
    total = tsend[f]
    for n in range(1, 32):
        t1_copies[n - 1].wait_recv()
        total = total + trecv[n]
    tbuf[z] = total
    t2_copies = []
    for k in range(1, 16):
        copy = remote(tbuf.at[z], tbuf.at[z], t2_send.at[k], t2_recv.at[k], z_peers[k - 1])
        copy.start()
        t2_copies.append(copy)

    total = psend[f]
    for k in range(1, 8):
        p_copies[k - 1].wait_recv()
        total = total + precv[k]
    proj_out[...] = total
    for copy in q_copies + g_copies + sent + e_copies + e2_copies + p_copies + t1_copies:
        copy.wait_send()
    for copy in e2_copies:
        copy.wait_recv()
    for copy in t2_copies:
        copy.wait()

    emb_all = ebuf[...].reshape(128, 128)
    grad_all = tbuf[...].reshape(128, 128)
    in_high = lax.broadcasted_iota(jnp.int32, (128, 128), 0) % 8 >= 4
    for half in range(2):
        ours = jnp.where(in_high if half else jnp.logical_not(in_high), grad_all, 0.0)
        for k_half in range(2):
            rows = emb_all
            if k_half != half:
                rows = pltpu.roll(emb_all, 4 if half else 124, 0)
            gwg_out[128 * k_half : 128 * k_half + 128, 128 * half : 128 * half + 128] = (
                lax.dot_general(
                    rows, ours, (((0,), (0,)), ((), ())),
                    precision=lax.Precision.HIGHEST, preferred_element_type=F32,
                ) * (8 * 192 * 64) ** (-0.5)
            )
    store_mixed.wait()
    store_grads.wait()


def frequency_embedding(step_values, freq_width):
    half_width = freq_width // 2
    counter = jnp.arange(half_width, dtype=jnp.float32)
    frequencies = jnp.exp(-jnp.log(10000.0) * counter / half_width)
    angles = step_values.astype(jnp.float32)[:, None] * frequencies[None, :]
    return jnp.concatenate([jnp.cos(angles), jnp.sin(angles)], axis=-1)


def per_device(
    values, cotangent, out_weight, gate_weight, in_probe, out_probe, timesteps, text_lengths
):
    embedding = frequency_embedding(timesteps, 256)
    vmem = pl.BlockSpec(memory_space=pltpu.VMEM)
    smem = pl.BlockSpec(memory_space=pltpu.SMEM)
    anywhere = pl.BlockSpec(memory_space=pltpu.HBM)
    dma = pltpu.SemaphoreType.DMA
    count = OWN + 1
    mixed, grads, projected, gwg = pl.pallas_call(
        kernel,
        out_shape=(
            jax.ShapeDtypeStruct((192, 2048), BF16),
            jax.ShapeDtypeStruct((192, 2048), BF16),
            jax.ShapeDtypeStruct((8, 64), F32),
            jax.ShapeDtypeStruct((256, 256), F32),
        ),
        in_specs=[vmem, vmem, smem, anywhere, anywhere, anywhere, anywhere, anywhere],
        out_specs=(anywhere, anywhere, vmem, vmem),
        scratch_shapes=[
            pltpu.VMEM((2048, 2048), BF16),
            pltpu.VMEM((192, 2048), BF16),
            pltpu.VMEM((192, 2048), BF16),
            pltpu.VMEM((64, 2048), BF16),
            pltpu.VMEM((64, 2048), BF16),
            pltpu.VMEM((256, 256), BF16),
            pltpu.VMEM((192, 2048), BF16),
            pltpu.VMEM((128, 128), BF16),
            pltpu.VMEM((192, 2048), BF16),
            pltpu.VMEM((192, 2048), BF16),
            pltpu.VMEM((192, 2048), BF16),
            pltpu.VMEM((192, 2048), F32),
            pltpu.VMEM((8, 2048), F32),
            pltpu.VMEM((4, 16, 512), BF16),
            pltpu.VMEM((8, 8, 64), F32),
            pltpu.VMEM((8, 8, 64), F32),
            pltpu.VMEM((8, 128), F32),
            pltpu.VMEM((4, 8, 128), F32),
            pltpu.VMEM((16, 8, 128), F32),
            pltpu.VMEM((8, 8, 128), F32),
            pltpu.VMEM((32, 8, 128), F32),
            pltpu.VMEM((16, 8, 128), F32),
            dma((7,)),
            dma((4,)), dma((4,)),
            dma((8,)), dma((8,)),
            dma((8,)), dma((8,)),
            dma((H, count)), dma((H, count)),
            dma((H, count)), dma((H, count)),
            dma((8,)), dma((8,)),
            dma((4,)), dma((4,)),
            dma((16,)), dma((16,)),
            dma((32,)), dma((32,)),
            dma((16,)), dma((16,)),
        ],
        compiler_params=pltpu.CompilerParams(
            collective_id=0, has_side_effects=True, vmem_limit_bytes=40 * 1024 * 1024
        ),
        cost_estimate=pl.CostEstimate(
            flops=4 * 192 * 2048 * 2048, bytes_accessed=8 * 192 * 2048, transcendentals=0
        ),
    )(
        out_weight, embedding, text_lengths, gate_weight,
        values[0], cotangent[0], in_probe.T, out_probe.T,
    )
    return mixed[None], grads[None], projected[None], gwg


def solution(mesh):
    in_specs = (
        P("dp", "fsdp", None),
        P("dp", "fsdp", None),
        P(("fsdp", "dp"), None),
        P(None, "fsdp"),
        P(),
        P(),
        P("dp"),
        P("dp"),
    )
    out_specs = (
        P("dp", "fsdp", None),
        P("dp", "fsdp", None),
        P("dp", "fsdp", None),
        P(None, "fsdp"),
    )
    return jax.shard_map(
        per_device, mesh=mesh, in_specs=in_specs, out_specs=out_specs, check_vma=False
    )
```

```python
import jax
import jax.numpy as jnp
from jax import lax
from jax.experimental import pallas as pl
from jax.experimental.pallas import tpu as pltpu
from jax.sharding import PartitionSpec as P

MESH = pl.DeviceIdType.MESH
F32, BF16 = jnp.float32, jnp.bfloat16
TXT = 256
GROUPS = ((0, 48), (48, 80))
SLOTS = ((1, 2), (3, 4, 5, 6, 7))
H = len(GROUPS)
FAR_FIRST = (8, 7, 9, 6, 10, 5, 11, 4, 12, 3, 13, 2, 14, 1, 15)
VMEM_BYTES = 63 * 1024 * 1024

AXIS = [(-1, 0), (0, -1), (1, 0), (0, 1), (2, 0), (0, 2)]
FORWARDED = [(i, -1, "A") for i in (-1, 1, 2)] + [(-1, j, "B") for j in (-1, 1, 2)]
FORWARDED = [FORWARDED[n] for n in (0, 3, 1, 4, 2, 5)]
FINAL = [(i, j, "A") for j in (1, 2) for i in (-1, 1, 2)] + [
    (i, j, "B") for i in (1, 2) for j in (-1, 1, 2)
]
FINAL = [FINAL[n] for n in (0, 6, 1, 7, 2, 8, 3, 9, 4, 10, 5, 11)]
SIDE = [message for message in FINAL if message[:2] in ((-1, 1), (1, 1), (1, -1), (1, 2), (2, 1))]
SIDE = [message for message in SIDE if message not in ((1, 2, "A"), (2, 1, "B"))]
LAST = [message for message in FINAL if message not in SIDE]
MESSAGES = [(i, j, "AB") for i, j in AXIS] + FORWARDED + FINAL
INDEX = {message: n for n, message in enumerate(MESSAGES)}
OWN = len(MESSAGES)


def onward(message):
    i, j, part = message
    if part == "A":
        return [("yf", (i, 2, "A"))] if j == -1 else []
    if part == "B":
        return [("xf", (2, j, "B"))] if i == -1 else []
    if (i, j) == (0, 0):
        return [
            ("xf", (-1, 0, "AB")), ("yf", (0, -1, "AB")),
            ("xb", (1, 0, "AB")), ("yb", (0, 1, "AB")),
        ]
    if j == 0:
        first = [("xf", (2, 0, "AB"))] if i == -1 else []
        return first + [("yf", (i, -1, "A")), ("yb", (i, 1, "A"))]
    first = [("yf", (0, 2, "AB"))] if j == -1 else []
    return first + [("xf", (-1, j, "B")), ("xb", (1, j, "B"))]


def kernel(
    w_ref, emb_ref, len_ref, gw_ref, values_ref, cot_ref, inp_ref, outp_ref,
    mixed_out, grads_out, proj_out, gwg_out,
    wbuf, vals, cot, inp, outp, gw, valsp, place, masked, mixed, grads, gradsp, left, acc, gate,
    qbuf, psend, precv, eown, erecv, ebuf, tsend, trecv, tbuf,
    l_sem, q_send, q_recv, g_send, g_recv, z_send, z_recv, x_send, x_recv, d_send, d_recv,
    far_sem, p_send, p_recv, e1_send, e1_recv, e2_send, e2_recv, t1_send, t1_recv, t2_send, t2_recv,
):
    f, d = lax.axis_index("fsdp"), lax.axis_index("dp")
    x_lo, y = f // 4, f % 4
    x_hi, z, c = d // 32, (d // 2) % 16, d % 2
    x = 2 * x_hi + x_lo
    s = 1 - 2 * c
    m, p = z // 2, z % 2

    def device(xx, yy, zz, cc):
        return ((xx % 2) * 4 + yy, (xx // 2) * 32 + zz * 2 + cc)

    def remote(src, dst, send, recv, target):
        return pltpu.make_async_remote_copy(
            src_ref=src, dst_ref=dst, send_sem=send, recv_sem=recv,
            device_id=target, device_id_type=MESH,
        )

    loads = [
        pltpu.make_async_copy(a, b, l_sem.at[n])
        for n, (a, b) in enumerate(
            ((gw_ref, gw), (values_ref, vals), (cot_ref, cot), (inp_ref, inp), (outp_ref, outp))
        )
    ]
    for load in loads:
        load.start()

    here = (f, d)
    core_peer = device(x, y, z, 1 - c)
    z_peers = [device(x, y, (z + k) % 16, c) for k in range(1, 16)]
    f_peers = [((f + k) % 8, d) for k in range(1, 8)]
    quad_peers = []
    for k in range(1, 4):
        t = (2 * x_hi + c + k) % 4
        quad_peers.append((f, (t // 2) * 32 + z * 2 + t % 2))
    way = {
        "xf": device((x + s + 4) % 4, y, z, c),
        "xb": device((x - s + 4) % 4, y, z, c),
        "yf": device(x, (y + s + 4) % 4, z, c),
        "yb": device(x, (y - s + 4) % 4, z, c),
    }

    barrier = pltpu.get_barrier_semaphore()
    greeted = [z_peers[k - 1] for k in (4, 12, 3, 13, 2, 14, 1, 15)] + f_peers + quad_peers
    greeted = greeted + [
        (f, x_hi * 32 + (z + 1 - 2 * p) * 2 + 1 - c),
        ((1 - x_lo) * 4 + y, (1 - x_hi) * 32 + z * 2 + c),
    ]
    for peer in greeted:
        pl.semaphore_signal(barrier, inc=1, device_id=peer, device_id_type=MESH)

    mine = w_ref[...].astype(F32)
    t_own = 2 * p + c
    qbuf[t_own] = jnp.concatenate(
        [mine[:, 512 * n : 512 * n + 512] for n in range(4)], axis=0
    ).astype(BF16)
    pl.semaphore_wait(barrier, len(greeted))
    for k in (4, 12):
        pl.semaphore_signal(far_sem, inc=1, device_id=z_peers[k - 1], device_id_type=MESH)

    q_copies = []
    for k in range(1, 4):
        t = (t_own + k) % 4
        target = device(x, y, 2 * m + t // 2, t % 2)
        copy = remote(qbuf.at[t_own], qbuf.at[t_own], q_send.at[k], q_recv.at[k], target)
        copy.start()
        q_copies.append(copy)

    emb = emb_ref[...]
    loads[0].wait()
    share = jnp.dot(
        jnp.broadcast_to(emb, (8, 256)), gw[...].astype(F32),
        precision=lax.Precision.HIGHEST, preferred_element_type=F32,
    )
    f_cols = pl.ds(pl.multiple_of(256 * f, 256), 256)
    gate[:, f_cols] = share
    g_copies = []
    for k in range(1, 8):
        copy = remote(gate.at[:, f_cols], gate.at[:, f_cols], g_send.at[k], g_recv.at[k], f_peers[k - 1])
        copy.start()
        g_copies.append(copy)

    for copy in q_copies:
        copy.wait_recv()
    quarter = [qbuf[t].astype(F32) for t in range(4)]
    low, high = [
        jnp.concatenate(
            [
                jnp.concatenate([quarter[t][4 * n : 4 * n + 4] for t in range(4)], axis=0)
                for n in pair
            ],
            axis=1,
        )
        for pair in ((0, 1), (2, 3))
    ]

    def row_of(i, j):
        xx, yy = (x + s * i + 8) % 4, (y + s * j + 8) % 4
        return (xx % 2) * 1024 + yy * 256 + (xx // 2) * 128

    def cols_of(core, part):
        start = 1024 * core + (512 if part == "B" else 0)
        return pl.ds(pl.multiple_of(start, 512), 1024 if part == "AB" else 512)

    own = row_of(0, 0)
    own_rows = pl.ds(pl.multiple_of(own, 16), 16)
    half_cols = cols_of(c, "AB")
    wbuf[own_rows, half_cols] = jnp.where(c == 0, low, high).astype(BF16)

    sent = []
    for k in range(1, 8):
        if k == 5:
            pl.semaphore_wait(far_sem, 2)
        away = (k + 1) // 2
        slot = 2 * away - 1 + (p if away < 4 else 0)
        there = pl.ds(pl.multiple_of(own + 16 * slot, 16), 16)
        copy = remote(
            wbuf.at[own_rows, half_cols], wbuf.at[there, half_cols], z_send.at[k], z_recv.at[slot],
            device(x, y, (z + (2 * p - 1) * k + 16) % 16, c),
        )
        copy.start()
        sent.append(copy)

    def z_wait(h):
        for slot in SLOTS[h]:
            block = wbuf.at[pl.ds(pl.multiple_of(own + 16 * slot, 16), 16), half_cols]
            remote(block, block, z_send.at[slot], z_recv.at[slot], core_peer).wait_recv()

    def block_of(core, h, message):
        i, j, part = message
        first, count = GROUPS[h]
        rows = pl.ds(pl.multiple_of(row_of(i, j) + first, 16), count)
        return wbuf.at[rows, cols_of(core, part)]


    def part_block(h, message, part):
        return block_of(c, h, (message[0], message[1], part))

    def forward(h, message):
        i, j, part = message
        for direction, there in onward(message):
            n = INDEX[there]
            block = part_block(h, message, there[2])
            copy = remote(block, block, x_send.at[h, n], x_recv.at[h, n], way[direction])
            copy.start()
            sent.append(copy)
        n = OWN if (i, j) == (0, 0) else INDEX[message]
        block = block_of(c, h, message)
        copy = remote(block, block, d_send.at[h, n], d_recv.at[h, n], core_peer)
        copy.start()
        sent.append(copy)

    def take(h, message):
        n = INDEX[message]
        block = block_of(c, h, message)
        remote(block, block, x_send.at[h, n], x_recv.at[h, n], core_peer).wait_recv()
        forward(h, message)

    def from_other_core(i, j):
        i_there, j_there = (-i if i % 2 else i), (-j if j % 2 else j)
        for h in range(H):
            for part in ("AB",) if 0 in (i, j) else ("A", "B"):
                n = OWN if (i, j) == (0, 0) else INDEX[(i_there, j_there, part)]
                block = block_of(1 - c, h, (i, j, part))
                remote(block, block, d_send.at[h, n], d_recv.at[h, n], core_peer).wait_recv()

    e = 2 * x_hi + c
    tile_row = lax.broadcasted_iota(jnp.int32, (8, 128), 0)

    def tile_of(row):
        low = jnp.broadcast_to(row[:, :128], (8, 128))
        high = jnp.broadcast_to(row[:, 128:], (8, 128))
        zero = jnp.zeros((8, 128), F32)
        return jnp.where(tile_row == e, low, jnp.where(tile_row == e + 4, high, zero))

    eown[...] = tile_of(emb)
    e_copies = []
    for k in range(1, 4):
        copy = remote(eown, erecv.at[k], e1_send.at[k], e1_recv.at[k], quad_peers[k - 1])
        copy.start()
        e_copies.append(copy)

    k_at = lax.broadcasted_iota(jnp.int32, (128, 128), 0)
    n_at = lax.broadcasted_iota(jnp.int32, (128, 128), 1)
    slot_at = n_at // 16
    away_at = jnp.where(slot_at % 2 == 1, (slot_at + 1) // 2, 8 - slot_at // 2)
    place[...] = jnp.where(k_at == (m + away_at) % 8 * 16 + n_at % 16, 1.0, 0.0).astype(BF16)

    for load in loads[1:]:
        load.wait()
    for n in range(16):
        cols = slice(128 * n, 128 * n + 128)
        valsp[:, cols] = jnp.dot(
            vals[:, cols], place[...], preferred_element_type=F32
        ).astype(BF16)

    z_wait(0)
    forward(0, (0, 0, "AB"))

    for copy in g_copies:
        copy.wait_recv()
    limit = 8 * 192 - TXT + len_ref[0]

    def valid(width):
        return lax.broadcasted_iota(jnp.int32, (192, width), 0) + f * 192 < limit

    @pl.loop(0, 8)
    def _(n):
        cols = pl.ds(pl.multiple_of(n * 256, 256), 256)
        scaled = jnp.where(valid(256), cot[:, cols].astype(F32), 0.0)
        masked[:, cols] = (scaled * gate[0:1, cols]).astype(BF16)

    for i, j in AXIS:
        take(0, (i, j, "AB"))
    z_wait(1)
    forward(1, (0, 0, "AB"))
    for message in FORWARDED:
        take(0, message)

    for copy in e_copies:
        copy.wait_recv()
    ebuf[z] = eown[...] + erecv[1] + erecv[2] + erecv[3]
    e2_copies = []
    for k in FAR_FIRST:
        copy = remote(ebuf.at[z], ebuf.at[z], e2_send.at[k], e2_recv.at[k], z_peers[k - 1])
        copy.start()
        e2_copies.append(copy)

    for i, j in AXIS:
        take(1, (i, j, "AB"))

    turned = (((1,), (1,)), ((), ()))
    probe_in = lax.dot_general(vals[...], inp[...], turned, preferred_element_type=F32).astype(BF16)
    probe_out = lax.dot_general(masked[...], outp[...], turned, preferred_element_type=F32).astype(BF16)
    projected = lax.dot_general(
        probe_in, probe_out, (((0,), (0,)), ((), ())), preferred_element_type=F32
    ) * (8 * 192) ** (-0.5)
    psend[...] = projected.reshape(8, 8, 64)
    p_copies = []
    for k in range(1, 8):
        copy = remote(psend.at[(f + k) % 8], precv.at[k], p_send.at[k], p_recv.at[k], f_peers[k - 1])
        copy.start()
        p_copies.append(copy)

    for message in FINAL:
        take(0, message)

    def pair_rows(i, j):
        xx, yy = (x + i + 8) % 2, (y + s * j + 8) % 4
        return pl.ds(pl.multiple_of(xx * 1024 + yy * 256, 256), 256)

    def branch(i, j, first=False):
        rows = pair_rows(i, j)

        product = jnp.dot(valsp[:, rows], wbuf[rows, :], preferred_element_type=F32)
        acc[...] = product if first else acc[...] + product

    def grad(i, j):
        rows = pair_rows(i, j)
        gradsp[:, rows] = lax.dot_general(
            masked[...], wbuf[rows, :], turned, preferred_element_type=F32
        ).astype(BF16)

    def pair_wait(i, j):
        for i_each in (0, 2) if i == 0 else (-1, 1):
            from_other_core(i_each, j)

    for message in FORWARDED:
        take(1, message)
    pair_wait(0, 0)
    branch(0, 0, first=True)
    pair_wait(1, 0)
    branch(1, 0)
    for message in SIDE:
        take(1, message)
    for j in (-1, 1):
        pair_wait(1, j)
        branch(1, j)
    grad(0, 0)
    grad(1, 0)
    for message in LAST:
        take(1, message)
    for i, j in ((0, -1), (0, 1), (1, 2), (0, 2)):
        pair_wait(i, j)
        branch(i, j)

    for n in range(8):
        cols = slice(256 * n, 256 * n + 256)
        scaled = jnp.where(valid(256), cot[:, cols].astype(F32), 0.0)
        tsend[n] = tile_of(jnp.sum(scaled * acc[:, cols], axis=0, keepdims=True))

    t1_copies = {}
    for n in sorted(range(1, 32), key=lambda n: -(n // 4 in (2, 6)) - (n % 4 in (1, 2, 3))):
        to_f, t = (f + n // 4) % 8, (e + n % 4) % 4
        copy = remote(
            tsend.at[to_f], trecv.at[n], t1_send.at[n], t1_recv.at[n],
            (to_f, (t // 2) * 32 + z * 2 + t % 2),
        )
        copy.start()
        t1_copies[n] = copy
    for n in range(8):
        cols = slice(256 * n, 256 * n + 256)
        mixed[:, cols] = (acc[:, cols] * gate[0:1, cols]).astype(BF16)
    store_mixed = pltpu.make_async_copy(mixed, mixed_out, l_sem.at[5])
    store_mixed.start()
    for i, j in ((1, -1), (1, 1), (0, -1)):
        grad(i, j)
    total = tsend[f]
    for n in range(1, 32):
        t1_copies[n].wait_recv()
        total = total + trecv[n]
    tbuf[z] = total
    t2_copies = []
    for k in FAR_FIRST:
        copy = remote(tbuf.at[z], tbuf.at[z], t2_send.at[k], t2_recv.at[k], z_peers[k - 1])
        copy.start()
        t2_copies.append(copy)
    for i, j in ((0, 1), (1, 2), (0, 2)):
        grad(i, j)
    for n in range(16):
        cols = slice(128 * n, 128 * n + 128)
        grads[:, cols] = lax.dot_general(
            gradsp[:, cols], place[...], turned, preferred_element_type=F32
        ).astype(BF16)
    store_grads = pltpu.make_async_copy(grads, grads_out, l_sem.at[6])
    store_grads.start()

    for copy in e2_copies:
        copy.wait_recv()
    emb_all = ebuf[...].reshape(128, 128) * (8 * 192 * 64) ** (-0.5)
    in_high = lax.broadcasted_iota(jnp.int32, (128, 128), 0) % 8 >= 4
    for half in range(2):
        for k_half in range(2):
            rows = emb_all
            if k_half != half:
                rows = pltpu.roll(emb_all, 4 if half else 124, 0)
            rows = jnp.where(in_high if half else jnp.logical_not(in_high), rows, 0.0)
            left[half, 128 * k_half : 128 * k_half + 128, :] = rows.T

    total = psend[f]
    for k in range(1, 8):
        p_copies[k - 1].wait_recv()
        total = total + precv[k]
    proj_out[...] = total
    for copy in q_copies + g_copies + sent + e_copies + e2_copies + p_copies + list(t1_copies.values()):
        copy.wait_send()
    for copy in t2_copies:
        copy.wait()
    grad_all = tbuf[...].reshape(128, 128)
    for half in range(2):
        gwg_out[:, 128 * half : 128 * half + 128] = jnp.dot(
            left[half], grad_all, precision=lax.Precision.HIGHEST, preferred_element_type=F32
        )
    store_mixed.wait()
    store_grads.wait()


def frequency_embedding(step_values, freq_width):
    half_width = freq_width // 2
    counter = jnp.arange(half_width, dtype=jnp.float32)
    frequencies = jnp.exp(-jnp.log(10000.0) * counter / half_width)
    angles = step_values.astype(jnp.float32)[:, None] * frequencies[None, :]
    return jnp.concatenate([jnp.cos(angles), jnp.sin(angles)], axis=-1)


def per_device(
    values, cotangent, out_weight, gate_weight, in_probe, out_probe, timesteps, text_lengths
):
    embedding = frequency_embedding(timesteps, 256)
    vmem = pl.BlockSpec(memory_space=pltpu.VMEM)
    smem = pl.BlockSpec(memory_space=pltpu.SMEM)
    anywhere = pl.BlockSpec(memory_space=pltpu.HBM)
    dma = pltpu.SemaphoreType.DMA
    count = OWN + 1
    mixed, grads, projected, gwg = pl.pallas_call(
        kernel,
        out_shape=(
            jax.ShapeDtypeStruct((192, 2048), BF16),
            jax.ShapeDtypeStruct((192, 2048), BF16),
            jax.ShapeDtypeStruct((8, 64), F32),
            jax.ShapeDtypeStruct((256, 256), F32),
        ),
        in_specs=[vmem, vmem, smem, anywhere, anywhere, anywhere, anywhere, anywhere],
        out_specs=(anywhere, anywhere, vmem, vmem),
        scratch_shapes=[
            pltpu.VMEM((2048, 2048), BF16),
            pltpu.VMEM((192, 2048), BF16),
            pltpu.VMEM((192, 2048), BF16),
            pltpu.VMEM((64, 2048), BF16),
            pltpu.VMEM((64, 2048), BF16),
            pltpu.VMEM((256, 256), BF16),
            pltpu.VMEM((192, 2048), BF16),
            pltpu.VMEM((128, 128), BF16),
            pltpu.VMEM((192, 2048), BF16),
            pltpu.VMEM((192, 2048), BF16),
            pltpu.VMEM((192, 2048), BF16),
            pltpu.VMEM((192, 2048), BF16),
            pltpu.VMEM((2, 256, 128), F32),
            pltpu.VMEM((192, 2048), F32),
            pltpu.VMEM((8, 2048), F32),
            pltpu.VMEM((4, 16, 512), BF16),
            pltpu.VMEM((8, 8, 64), F32),
            pltpu.VMEM((8, 8, 64), F32),
            pltpu.VMEM((8, 128), F32),
            pltpu.VMEM((4, 8, 128), F32),
            pltpu.VMEM((16, 8, 128), F32),
            pltpu.VMEM((8, 8, 128), F32),
            pltpu.VMEM((32, 8, 128), F32),
            pltpu.VMEM((16, 8, 128), F32),
            dma((7,)),
            dma((4,)), dma((4,)),
            dma((8,)), dma((8,)),
            dma((8,)), dma((8,)),
            dma((H, count)), dma((H, count)),
            dma((H, count)), dma((H, count)),
            pltpu.SemaphoreType.REGULAR,
            dma((8,)), dma((8,)),
            dma((4,)), dma((4,)),
            dma((16,)), dma((16,)),
            dma((32,)), dma((32,)),
            dma((16,)), dma((16,)),
        ],
        compiler_params=pltpu.CompilerParams(
            collective_id=0, has_side_effects=True, vmem_limit_bytes=VMEM_BYTES
        ),
        cost_estimate=pl.CostEstimate(
            flops=4 * 192 * 2048 * 2048, bytes_accessed=8 * 192 * 2048, transcendentals=0
        ),
    )(
        out_weight, embedding, text_lengths, gate_weight,
        values[0], cotangent[0], in_probe.T, out_probe.T,
    )
    return mixed[None], grads[None], projected[None], gwg


def solution(mesh):
    in_specs = (
        P("dp", "fsdp", None),
        P("dp", "fsdp", None),
        P(("fsdp", "dp"), None),
        P(None, "fsdp"),
        P(),
        P(),
        P("dp"),
        P("dp"),
    )
    out_specs = (
        P("dp", "fsdp", None),
        P("dp", "fsdp", None),
        P("dp", "fsdp", None),
        P(None, "fsdp"),
    )
    return jax.shard_map(
        per_device, mesh=mesh, in_specs=in_specs, out_specs=out_specs, check_vma=False
    )
```

```python
import jax
import jax.numpy as jnp
from jax import lax
from jax.experimental import pallas as pl
from jax.experimental.pallas import tpu as pltpu
from jax.sharding import PartitionSpec as P

MESH = pl.DeviceIdType.MESH
F32, BF16 = jnp.float32, jnp.bfloat16
TXT = 256
GROUPS = ((0, 16), (16, 32), (48, 80))
H = len(GROUPS)
FAR_FIRST = (8, 7, 9, 6, 10, 5, 11, 4, 12, 3, 13, 2, 14, 1, 15)
VMEM_BYTES = 63 * 1024 * 1024

AXIS = [(-1, 0), (0, -1), (1, 0), (0, 1), (2, 0), (0, 2)]
FORWARDED = [(i, -1, "A") for i in (-1, 1, 2)] + [(-1, j, "B") for j in (-1, 1, 2)]
FORWARDED = [FORWARDED[n] for n in (0, 3, 1, 4, 2, 5)]
FINAL = [(i, j, "A") for j in (1, 2) for i in (-1, 1, 2)] + [
    (i, j, "B") for i in (1, 2) for j in (-1, 1, 2)
]
FINAL = [FINAL[n] for n in (0, 6, 1, 7, 2, 8, 3, 9, 4, 10, 5, 11)]
SIDE = [message for message in FINAL if message[:2] in ((-1, 1), (1, 1), (1, -1), (1, 2), (2, 1))]
SIDE = [message for message in SIDE if message not in ((1, 2, "A"), (2, 1, "B"))]
LAST = [message for message in FINAL if message not in SIDE]
MESSAGES = [(i, j, "AB") for i, j in AXIS] + FORWARDED + FINAL
INDEX = {message: n for n, message in enumerate(MESSAGES)}
OWN = len(MESSAGES)


def onward(message):
    i, j, part = message
    if part == "A":
        return [("yf", (i, 2, "A"))] if j == -1 else []
    if part == "B":
        return [("xf", (2, j, "B"))] if i == -1 else []
    if (i, j) == (0, 0):
        return [
            ("xf", (-1, 0, "AB")), ("yf", (0, -1, "AB")),
            ("xb", (1, 0, "AB")), ("yb", (0, 1, "AB")),
        ]
    if j == 0:
        first = [("xf", (2, 0, "AB"))] if i == -1 else []
        return first + [("yf", (i, -1, "A")), ("yb", (i, 1, "A"))]
    first = [("yf", (0, 2, "AB"))] if j == -1 else []
    return first + [("xf", (-1, j, "B")), ("xb", (1, j, "B"))]


def kernel(
    w_ref, emb_ref, len_ref, gw_ref, values_ref, cot_ref, inp_ref, outp_ref,
    mixed_out, grads_out, proj_out, gwg_out,
    wbuf, vals, cot, inp, outp, gw, valsp, place, masked, mixed, grads, gradsp, left, acc, gate,
    qbuf, psend, precv, eown, erecv, ebuf, tsend, trecv, tbuf,
    l_sem, q_send, q_recv, g_send, g_recv, z_send, z_recv, x_send, x_recv, d_send, d_recv,
    p_send, p_recv, e1_send, e1_recv, e2_send, e2_recv, t1_send, t1_recv, t2_send, t2_recv,
):
    f, d = lax.axis_index("fsdp"), lax.axis_index("dp")
    x_lo, y = f // 4, f % 4
    x_hi, z, c = d // 32, (d // 2) % 16, d % 2
    x = 2 * x_hi + x_lo
    s = 1 - 2 * c
    m, p = z // 2, z % 2

    def device(xx, yy, zz, cc):
        return ((xx % 2) * 4 + yy, (xx // 2) * 32 + zz * 2 + cc)

    def remote(src, dst, send, recv, target):
        return pltpu.make_async_remote_copy(
            src_ref=src, dst_ref=dst, send_sem=send, recv_sem=recv,
            device_id=target, device_id_type=MESH,
        )

    loads = [
        pltpu.make_async_copy(a, b, l_sem.at[n])
        for n, (a, b) in enumerate(
            ((gw_ref, gw), (values_ref, vals), (cot_ref, cot), (inp_ref, inp), (outp_ref, outp))
        )
    ]
    for load in loads:
        load.start()

    here = (f, d)
    core_peer = device(x, y, z, 1 - c)
    z_peers = [device(x, y, (z + k) % 16, c) for k in range(1, 16)]
    f_peers = [((f + k) % 8, d) for k in range(1, 8)]
    quad_peers = []
    for k in range(1, 4):
        t = (2 * x_hi + c + k) % 4
        quad_peers.append((f, (t // 2) * 32 + z * 2 + t % 2))
    way = {
        "xf": device((x + s + 4) % 4, y, z, c),
        "xb": device((x - s + 4) % 4, y, z, c),
        "yf": device(x, (y + s + 4) % 4, z, c),
        "yb": device(x, (y - s + 4) % 4, z, c),
    }

    barrier = pltpu.get_barrier_semaphore()
    greeted = [z_peers[k - 1] for k in (4, 12, 3, 13, 2, 14, 1, 15)] + f_peers + quad_peers
    greeted = greeted + [
        (f, x_hi * 32 + (z + 1 - 2 * p) * 2 + 1 - c),
        ((1 - x_lo) * 4 + y, (1 - x_hi) * 32 + z * 2 + c),
    ]
    for peer in greeted:
        pl.semaphore_signal(barrier, inc=1, device_id=peer, device_id_type=MESH)

    mine = w_ref[...].astype(F32)
    t_own = 2 * p + c
    qbuf[t_own] = jnp.concatenate(
        [mine[:, 512 * n : 512 * n + 512] for n in range(4)], axis=0
    ).astype(BF16)
    pl.semaphore_wait(barrier, len(greeted))

    q_copies = []
    for k in range(1, 4):
        t = (t_own + k) % 4
        target = device(x, y, 2 * m + t // 2, t % 2)
        copy = remote(qbuf.at[t_own], qbuf.at[t_own], q_send.at[k], q_recv.at[k], target)
        copy.start()
        q_copies.append(copy)

    emb = emb_ref[...]
    loads[0].wait()
    share = jnp.dot(
        jnp.broadcast_to(emb, (8, 256)), gw[...].astype(F32),
        precision=lax.Precision.HIGHEST, preferred_element_type=F32,
    )
    f_cols = pl.ds(pl.multiple_of(256 * f, 256), 256)
    gate[:, f_cols] = share
    g_copies = []
    for k in range(1, 8):
        copy = remote(gate.at[:, f_cols], gate.at[:, f_cols], g_send.at[k], g_recv.at[k], f_peers[k - 1])
        copy.start()
        g_copies.append(copy)

    for copy in q_copies:
        copy.wait_recv()
    quarter = [qbuf[t].astype(F32) for t in range(4)]
    low, high = [
        jnp.concatenate(
            [
                jnp.concatenate([quarter[t][4 * n : 4 * n + 4] for t in range(4)], axis=0)
                for n in pair
            ],
            axis=1,
        )
        for pair in ((0, 1), (2, 3))
    ]

    def row_of(i, j):
        xx, yy = (x + s * i + 8) % 4, (y + s * j + 8) % 4
        return (xx % 2) * 1024 + yy * 256 + (xx // 2) * 128

    def cols_of(core, part):
        start = 1024 * core + (512 if part == "B" else 0)
        return pl.ds(pl.multiple_of(start, 512), 1024 if part == "AB" else 512)

    own = row_of(0, 0)
    own_rows = pl.ds(pl.multiple_of(own, 16), 16)
    half_cols = cols_of(c, "AB")
    wbuf[own_rows, half_cols] = jnp.where(c == 0, low, high).astype(BF16)

    sent = []

    def z_rows(slot):
        return pl.ds(pl.multiple_of(own + 16 * slot, 16), 16)

    def z_copy(k):
        away = (k + 1) // 2
        slot = 2 * away - 1 + (p if away < 4 else 0)
        source, hops = (own_rows, k) if k <= 4 else (z_rows(3 + p), k - 4)
        copy = remote(
            wbuf.at[source, half_cols], wbuf.at[z_rows(slot), half_cols], z_send.at[k],
            z_recv.at[slot], device(x, y, (z + (2 * p - 1) * hops + 16) % 16, c),
        )
        copy.start()
        sent.append(copy)

    def z_wait(slot):
        block = wbuf.at[z_rows(slot), half_cols]
        remote(block, block, z_send.at[slot], z_recv.at[slot], core_peer).wait_recv()

    for k in (4, 1, 2, 3):
        z_copy(k)

    def block_of(core, h, message):
        i, j, part = message
        first, count = GROUPS[h]
        rows = pl.ds(pl.multiple_of(row_of(i, j) + first, 16), count)
        return wbuf.at[rows, cols_of(core, part)]


    def part_block(h, message, part):
        return block_of(c, h, (message[0], message[1], part))

    def forward(h, message):
        i, j, part = message
        for direction, there in onward(message):
            n = INDEX[there]
            block = part_block(h, message, there[2])
            copy = remote(block, block, x_send.at[h, n], x_recv.at[h, n], way[direction])
            copy.start()
            sent.append(copy)
        n = OWN if (i, j) == (0, 0) else INDEX[message]
        block = block_of(c, h, message)
        copy = remote(block, block, d_send.at[h, n], d_recv.at[h, n], core_peer)
        copy.start()
        sent.append(copy)

    def take(h, message):
        n = INDEX[message]
        block = block_of(c, h, message)
        remote(block, block, x_send.at[h, n], x_recv.at[h, n], core_peer).wait_recv()
        forward(h, message)

    def from_other_core(i, j):
        i_there, j_there = (-i if i % 2 else i), (-j if j % 2 else j)
        for h in range(H):
            for part in ("AB",) if 0 in (i, j) else ("A", "B"):
                n = OWN if (i, j) == (0, 0) else INDEX[(i_there, j_there, part)]
                block = block_of(1 - c, h, (i, j, part))
                remote(block, block, d_send.at[h, n], d_recv.at[h, n], core_peer).wait_recv()

    forward(0, (0, 0, "AB"))
    e = 2 * x_hi + c
    tile_row = lax.broadcasted_iota(jnp.int32, (8, 128), 0)

    def tile_of(row):
        low = jnp.broadcast_to(row[:, :128], (8, 128))
        high = jnp.broadcast_to(row[:, 128:], (8, 128))
        zero = jnp.zeros((8, 128), F32)
        return jnp.where(tile_row == e, low, jnp.where(tile_row == e + 4, high, zero))

    eown[...] = tile_of(emb)
    e_copies = []
    for k in range(1, 4):
        copy = remote(eown, erecv.at[k], e1_send.at[k], e1_recv.at[k], quad_peers[k - 1])
        copy.start()
        e_copies.append(copy)

    k_at = lax.broadcasted_iota(jnp.int32, (128, 128), 0)
    n_at = lax.broadcasted_iota(jnp.int32, (128, 128), 1)
    slot_at = n_at // 16
    away_at = jnp.where(slot_at % 2 == 1, (slot_at + 1) // 2, 8 - slot_at // 2)
    place[...] = jnp.where(k_at == (m + away_at) % 8 * 16 + n_at % 16, 1.0, 0.0).astype(BF16)

    for load in loads[1:]:
        load.wait()
    for n in range(16):
        cols = slice(128 * n, 128 * n + 128)
        valsp[:, cols] = jnp.dot(
            vals[:, cols], place[...], preferred_element_type=F32
        ).astype(BF16)

    for slot in (1, 2):
        z_wait(slot)
    forward(1, (0, 0, "AB"))
    z_wait(3 + p)
    for k in (7, 6, 5):
        z_copy(k)

    for copy in g_copies:
        copy.wait_recv()
    limit = 8 * 192 - TXT + len_ref[0]

    def valid(width):
        return lax.broadcasted_iota(jnp.int32, (192, width), 0) + f * 192 < limit

    @pl.loop(0, 8)
    def _(n):
        cols = pl.ds(pl.multiple_of(n * 256, 256), 256)
        scaled = jnp.where(valid(256), cot[:, cols].astype(F32), 0.0)
        masked[:, cols] = (scaled * gate[0:1, cols]).astype(BF16)

    for h in range(2):
        for i, j in AXIS:
            take(h, (i, j, "AB"))
    for slot in (4 - p, 5, 6, 7):
        z_wait(slot)
    forward(2, (0, 0, "AB"))
    for h in range(2):
        for message in FORWARDED:
            take(h, message)

    for copy in e_copies:
        copy.wait_recv()
    ebuf[z] = eown[...] + erecv[1] + erecv[2] + erecv[3]
    e2_copies = []
    for k in FAR_FIRST:
        copy = remote(ebuf.at[z], ebuf.at[z], e2_send.at[k], e2_recv.at[k], z_peers[k - 1])
        copy.start()
        e2_copies.append(copy)

    for i, j in AXIS:
        take(2, (i, j, "AB"))

    turned = (((1,), (1,)), ((), ()))
    probe_in = lax.dot_general(vals[...], inp[...], turned, preferred_element_type=F32).astype(BF16)
    probe_out = lax.dot_general(masked[...], outp[...], turned, preferred_element_type=F32).astype(BF16)
    projected = lax.dot_general(
        probe_in, probe_out, (((0,), (0,)), ((), ())), preferred_element_type=F32
    ) * (8 * 192) ** (-0.5)
    psend[...] = projected.reshape(8, 8, 64)
    p_copies = []
    for k in range(1, 8):
        copy = remote(psend.at[(f + k) % 8], precv.at[k], p_send.at[k], p_recv.at[k], f_peers[k - 1])
        copy.start()
        p_copies.append(copy)

    for h in range(2):
        for message in FINAL:
            take(h, message)

    def pair_rows(i, j):
        xx, yy = (x + i + 8) % 2, (y + s * j + 8) % 4
        return pl.ds(pl.multiple_of(xx * 1024 + yy * 256, 256), 256)

    def branch(i, j, first=False):
        rows = pair_rows(i, j)

        product = jnp.dot(valsp[:, rows], wbuf[rows, :], preferred_element_type=F32)
        acc[...] = product if first else acc[...] + product

    def grad(i, j):
        rows = pair_rows(i, j)
        gradsp[:, rows] = lax.dot_general(
            masked[...], wbuf[rows, :], turned, preferred_element_type=F32
        ).astype(BF16)

    def pair_wait(i, j):
        for i_each in (0, 2) if i == 0 else (-1, 1):
            from_other_core(i_each, j)

    for message in FORWARDED:
        take(2, message)
    pair_wait(0, 0)
    branch(0, 0, first=True)
    pair_wait(1, 0)
    branch(1, 0)
    for message in SIDE:
        take(2, message)
    for j in (-1, 1):
        pair_wait(1, j)
        branch(1, j)
    grad(0, 0)
    grad(1, 0)
    for message in LAST:
        take(2, message)
    for i, j in ((0, -1), (0, 1), (1, 2), (0, 2)):
        pair_wait(i, j)
        branch(i, j)

    for n in range(8):
        cols = slice(256 * n, 256 * n + 256)
        scaled = jnp.where(valid(256), cot[:, cols].astype(F32), 0.0)
        tsend[n] = tile_of(jnp.sum(scaled * acc[:, cols], axis=0, keepdims=True))

    t1_copies = {}
    for n in sorted(range(1, 32), key=lambda n: -(n // 4 in (2, 6)) - (n % 4 in (1, 2, 3))):
        to_f, t = (f + n // 4) % 8, (e + n % 4) % 4
        copy = remote(
            tsend.at[to_f], trecv.at[n], t1_send.at[n], t1_recv.at[n],
            (to_f, (t // 2) * 32 + z * 2 + t % 2),
        )
        copy.start()
        t1_copies[n] = copy
    for n in range(8):
        cols = slice(256 * n, 256 * n + 256)
        mixed[:, cols] = (acc[:, cols] * gate[0:1, cols]).astype(BF16)
    store_mixed = pltpu.make_async_copy(mixed, mixed_out, l_sem.at[5])
    store_mixed.start()
    for i, j in ((1, -1), (1, 1), (0, -1)):
        grad(i, j)
    total = tsend[f]
    for n in range(1, 32):
        t1_copies[n].wait_recv()
        total = total + trecv[n]
    tbuf[z] = total
    t2_copies = []
    for k in FAR_FIRST:
        copy = remote(tbuf.at[z], tbuf.at[z], t2_send.at[k], t2_recv.at[k], z_peers[k - 1])
        copy.start()
        t2_copies.append(copy)
    for i, j in ((0, 1), (1, 2), (0, 2)):
        grad(i, j)
    for n in range(16):
        cols = slice(128 * n, 128 * n + 128)
        grads[:, cols] = lax.dot_general(
            gradsp[:, cols], place[...], turned, preferred_element_type=F32
        ).astype(BF16)
    store_grads = pltpu.make_async_copy(grads, grads_out, l_sem.at[6])
    store_grads.start()

    for copy in e2_copies:
        copy.wait_recv()
    emb_all = ebuf[...].reshape(128, 128) * (8 * 192 * 64) ** (-0.5)
    in_high = lax.broadcasted_iota(jnp.int32, (128, 128), 0) % 8 >= 4
    for half in range(2):
        for k_half in range(2):
            rows = emb_all
            if k_half != half:
                rows = pltpu.roll(emb_all, 4 if half else 124, 0)
            rows = jnp.where(in_high if half else jnp.logical_not(in_high), rows, 0.0)
            left[half, 128 * k_half : 128 * k_half + 128, :] = rows.T

    total = psend[f]
    for k in range(1, 8):
        p_copies[k - 1].wait_recv()
        total = total + precv[k]
    proj_out[...] = total
    for copy in q_copies + g_copies + sent + e_copies + e2_copies + p_copies + list(t1_copies.values()):
        copy.wait_send()
    for copy in t2_copies:
        copy.wait()
    grad_all = tbuf[...].reshape(128, 128)
    for half in range(2):
        gwg_out[:, 128 * half : 128 * half + 128] = jnp.dot(
            left[half], grad_all, precision=lax.Precision.HIGHEST, preferred_element_type=F32
        )
    store_mixed.wait()
    store_grads.wait()


def frequency_embedding(step_values, freq_width):
    half_width = freq_width // 2
    counter = jnp.arange(half_width, dtype=jnp.float32)
    frequencies = jnp.exp(-jnp.log(10000.0) * counter / half_width)
    angles = step_values.astype(jnp.float32)[:, None] * frequencies[None, :]
    return jnp.concatenate([jnp.cos(angles), jnp.sin(angles)], axis=-1)


def per_device(
    values, cotangent, out_weight, gate_weight, in_probe, out_probe, timesteps, text_lengths
):
    embedding = frequency_embedding(timesteps, 256)
    vmem = pl.BlockSpec(memory_space=pltpu.VMEM)
    smem = pl.BlockSpec(memory_space=pltpu.SMEM)
    anywhere = pl.BlockSpec(memory_space=pltpu.HBM)
    dma = pltpu.SemaphoreType.DMA
    count = OWN + 1
    mixed, grads, projected, gwg = pl.pallas_call(
        kernel,
        out_shape=(
            jax.ShapeDtypeStruct((192, 2048), BF16),
            jax.ShapeDtypeStruct((192, 2048), BF16),
            jax.ShapeDtypeStruct((8, 64), F32),
            jax.ShapeDtypeStruct((256, 256), F32),
        ),
        in_specs=[vmem, vmem, smem, anywhere, anywhere, anywhere, anywhere, anywhere],
        out_specs=(anywhere, anywhere, vmem, vmem),
        scratch_shapes=[
            pltpu.VMEM((2048, 2048), BF16),
            pltpu.VMEM((192, 2048), BF16),
            pltpu.VMEM((192, 2048), BF16),
            pltpu.VMEM((64, 2048), BF16),
            pltpu.VMEM((64, 2048), BF16),
            pltpu.VMEM((256, 256), BF16),
            pltpu.VMEM((192, 2048), BF16),
            pltpu.VMEM((128, 128), BF16),
            pltpu.VMEM((192, 2048), BF16),
            pltpu.VMEM((192, 2048), BF16),
            pltpu.VMEM((192, 2048), BF16),
            pltpu.VMEM((192, 2048), BF16),
            pltpu.VMEM((2, 256, 128), F32),
            pltpu.VMEM((192, 2048), F32),
            pltpu.VMEM((8, 2048), F32),
            pltpu.VMEM((4, 16, 512), BF16),
            pltpu.VMEM((8, 8, 64), F32),
            pltpu.VMEM((8, 8, 64), F32),
            pltpu.VMEM((8, 128), F32),
            pltpu.VMEM((4, 8, 128), F32),
            pltpu.VMEM((16, 8, 128), F32),
            pltpu.VMEM((8, 8, 128), F32),
            pltpu.VMEM((32, 8, 128), F32),
            pltpu.VMEM((16, 8, 128), F32),
            dma((7,)),
            dma((4,)), dma((4,)),
            dma((8,)), dma((8,)),
            dma((8,)), dma((8,)),
            dma((H, count)), dma((H, count)),
            dma((H, count)), dma((H, count)),
            dma((8,)), dma((8,)),
            dma((4,)), dma((4,)),
            dma((16,)), dma((16,)),
            dma((32,)), dma((32,)),
            dma((16,)), dma((16,)),
        ],
        compiler_params=pltpu.CompilerParams(
            collective_id=0, has_side_effects=True, vmem_limit_bytes=VMEM_BYTES
        ),
        cost_estimate=pl.CostEstimate(
            flops=4 * 192 * 2048 * 2048, bytes_accessed=8 * 192 * 2048, transcendentals=0
        ),
    )(
        out_weight, embedding, text_lengths, gate_weight,
        values[0], cotangent[0], in_probe.T, out_probe.T,
    )
    return mixed[None], grads[None], projected[None], gwg


def solution(mesh):
    in_specs = (
        P("dp", "fsdp", None),
        P("dp", "fsdp", None),
        P(("fsdp", "dp"), None),
        P(None, "fsdp"),
        P(),
        P(),
        P("dp"),
        P("dp"),
    )
    out_specs = (
        P("dp", "fsdp", None),
        P("dp", "fsdp", None),
        P("dp", "fsdp", None),
        P(None, "fsdp"),
    )
    return jax.shard_map(
        per_device, mesh=mesh, in_specs=in_specs, out_specs=out_specs, check_vma=False
    )
```

```python
import jax
import jax.numpy as jnp
from jax import lax
from jax.experimental import pallas as pl
from jax.experimental.pallas import tpu as pltpu
from jax.sharding import PartitionSpec as P

MESH = pl.DeviceIdType.MESH
F32, BF16 = jnp.float32, jnp.bfloat16
TXT = 256
GROUPS = ((0, 128),)
PIECES = ((0, 48), (48, 80))
H = len(GROUPS)
FAR_FIRST = (8, 7, 9, 6, 10, 5, 11, 4, 12, 3, 13, 2, 14, 1, 15)
VMEM_BYTES = 63 * 1024 * 1024

AXIS = [(-1, 0), (0, -1), (1, 0), (0, 1), (2, 0), (0, 2)]
FORWARDED = [(i, -1, "A") for i in (-1, 1, 2)] + [(-1, j, "B") for j in (-1, 1, 2)]
FORWARDED = [FORWARDED[n] for n in (0, 3, 1, 4, 2, 5)]
FINAL = [(i, j, "A") for j in (1, 2) for i in (-1, 1, 2)] + [
    (i, j, "B") for i in (1, 2) for j in (-1, 1, 2)
]
FINAL = [FINAL[n] for n in (0, 6, 1, 7, 2, 8, 3, 9, 4, 10, 5, 11)]
SIDE = [message for message in FINAL if message[:2] in ((-1, 1), (1, 1), (1, -1), (1, 2), (2, 1))]
SIDE = [message for message in SIDE if message not in ((1, 2, "A"), (2, 1, "B"))]
LAST = [message for message in FINAL if message not in SIDE]
MESSAGES = [(i, j, "AB") for i, j in AXIS] + FORWARDED + FINAL
INDEX = {message: n for n, message in enumerate(MESSAGES)}
OWN = len(MESSAGES)


def onward(message):
    i, j, part = message
    if part == "A":
        return [("yf", (i, 2, "A"))] if j == -1 else []
    if part == "B":
        return [("xf", (2, j, "B"))] if i == -1 else []
    if (i, j) == (0, 0):
        return [
            ("xf", (-1, 0, "AB")), ("yf", (0, -1, "AB")),
            ("xb", (1, 0, "AB")), ("yb", (0, 1, "AB")),
        ]
    if j == 0:
        first = [("xf", (2, 0, "AB"))] if i == -1 else []
        return first + [("yf", (i, -1, "A")), ("yb", (i, 1, "A"))]
    first = [("yf", (0, 2, "AB"))] if j == -1 else []
    return first + [("xf", (-1, j, "B")), ("xb", (1, j, "B"))]


def kernel(
    w_ref, emb_ref, len_ref, gw_ref, values_ref, cot_ref, inp_ref, outp_ref,
    mixed_out, grads_out, proj_out, gwg_out,
    wbuf, vals, cot, inp, outp, gw, valsp, place, masked, mixed, grads, gradsp, left, acc, gate,
    qbuf, psend, precv, eown, erecv, ebuf, tsend, trecv, tbuf,
    l_sem, q_send, q_recv, g_send, g_recv, z_send, z_recv, x_send, x_recv, d_send, d_recv, o_send, o_recv,
    p_send, p_recv, e1_send, e1_recv, e2_send, e2_recv, t1_send, t1_recv, t2_send, t2_recv,
):
    f, d = lax.axis_index("fsdp"), lax.axis_index("dp")
    x_lo, y = f // 4, f % 4
    x_hi, z, c = d // 32, (d // 2) % 16, d % 2
    x = 2 * x_hi + x_lo
    s = 1 - 2 * c
    m, p = z // 2, z % 2

    def device(xx, yy, zz, cc):
        return ((xx % 2) * 4 + yy, (xx // 2) * 32 + zz * 2 + cc)

    def remote(src, dst, send, recv, target):
        return pltpu.make_async_remote_copy(
            src_ref=src, dst_ref=dst, send_sem=send, recv_sem=recv,
            device_id=target, device_id_type=MESH,
        )

    loads = [
        pltpu.make_async_copy(a, b, l_sem.at[n])
        for n, (a, b) in enumerate(
            ((gw_ref, gw), (values_ref, vals), (cot_ref, cot), (inp_ref, inp), (outp_ref, outp))
        )
    ]
    for load in loads:
        load.start()

    here = (f, d)
    core_peer = device(x, y, z, 1 - c)
    z_peers = [device(x, y, (z + k) % 16, c) for k in range(1, 16)]
    f_peers = [((f + k) % 8, d) for k in range(1, 8)]
    quad_peers = []
    for k in range(1, 4):
        t = (2 * x_hi + c + k) % 4
        quad_peers.append((f, (t // 2) * 32 + z * 2 + t % 2))
    way = {
        "xf": device((x + s + 4) % 4, y, z, c),
        "xb": device((x - s + 4) % 4, y, z, c),
        "yf": device(x, (y + s + 4) % 4, z, c),
        "yb": device(x, (y - s + 4) % 4, z, c),
    }

    barrier = pltpu.get_barrier_semaphore()
    greeted = [z_peers[k - 1] for k in (4, 12, 3, 13, 2, 14, 1, 15)] + f_peers + quad_peers
    greeted = greeted + [
        (f, x_hi * 32 + (z + 1 - 2 * p) * 2 + 1 - c),
        ((1 - x_lo) * 4 + y, (1 - x_hi) * 32 + z * 2 + c),
    ]
    for peer in greeted:
        pl.semaphore_signal(barrier, inc=1, device_id=peer, device_id_type=MESH)

    mine = w_ref[...].astype(F32)
    t_own = 2 * p + c
    qbuf[t_own] = jnp.concatenate(
        [mine[:, 512 * n : 512 * n + 512] for n in range(4)], axis=0
    ).astype(BF16)
    pl.semaphore_wait(barrier, len(greeted))

    q_copies = []
    for k in range(1, 4):
        t = (t_own + k) % 4
        target = device(x, y, 2 * m + t // 2, t % 2)
        copy = remote(qbuf.at[t_own], qbuf.at[t_own], q_send.at[k], q_recv.at[k], target)
        copy.start()
        q_copies.append(copy)

    emb = emb_ref[...]
    loads[0].wait()
    share = jnp.dot(
        jnp.broadcast_to(emb, (8, 256)), gw[...].astype(F32),
        precision=lax.Precision.HIGHEST, preferred_element_type=F32,
    )
    f_cols = pl.ds(pl.multiple_of(256 * f, 256), 256)
    gate[:, f_cols] = share
    g_copies = []
    for k in range(1, 8):
        copy = remote(gate.at[:, f_cols], gate.at[:, f_cols], g_send.at[k], g_recv.at[k], f_peers[k - 1])
        copy.start()
        g_copies.append(copy)

    for copy in q_copies:
        copy.wait_recv()
    quarter = [qbuf[t].astype(F32) for t in range(4)]
    low, high = [
        jnp.concatenate(
            [
                jnp.concatenate([quarter[t][4 * n : 4 * n + 4] for t in range(4)], axis=0)
                for n in pair
            ],
            axis=1,
        )
        for pair in ((0, 1), (2, 3))
    ]

    def row_of(i, j):
        xx, yy = (x + s * i + 8) % 4, (y + s * j + 8) % 4
        return (xx % 2) * 1024 + yy * 256 + (xx // 2) * 128

    def cols_of(core, part):
        start = 1024 * core + (512 if part == "B" else 0)
        return pl.ds(pl.multiple_of(start, 512), 1024 if part == "AB" else 512)

    own = row_of(0, 0)
    own_rows = pl.ds(pl.multiple_of(own, 16), 16)
    half_cols = cols_of(c, "AB")
    wbuf[own_rows, half_cols] = jnp.where(c == 0, low, high).astype(BF16)

    sent = []

    def z_rows(slot):
        return pl.ds(pl.multiple_of(own + 16 * slot, 16), 16)

    def z_copy(k):
        away = (k + 1) // 2
        slot = 2 * away - 1 + (p if away < 4 else 0)
        source, hops = (own_rows, k) if k <= 4 else (z_rows(3 + p), k - 4)
        copy = remote(
            wbuf.at[source, half_cols], wbuf.at[z_rows(slot), half_cols], z_send.at[k],
            z_recv.at[slot], device(x, y, (z + (2 * p - 1) * hops + 16) % 16, c),
        )
        copy.start()
        sent.append(copy)

    def z_wait(slot):
        block = wbuf.at[z_rows(slot), half_cols]
        remote(block, block, z_send.at[slot], z_recv.at[slot], core_peer).wait_recv()

    for k in (4, 1, 2, 3):
        z_copy(k)

    def block_of(core, h, message):
        i, j, part = message
        first, count = GROUPS[h]
        rows = pl.ds(pl.multiple_of(row_of(i, j) + first, 16), count)
        return wbuf.at[rows, cols_of(core, part)]


    def own_piece(piece):
        first, count = PIECES[piece]
        block = wbuf.at[pl.ds(pl.multiple_of(own + first, 16), count), half_cols]
        for direction, there in onward((0, 0, "AB")):
            n = INDEX[there]
            copy = remote(block, block, o_send.at[piece, n], o_recv.at[piece, n], way[direction])
            copy.start()
            sent.append(copy)

    def part_block(h, message, part):
        return block_of(c, h, (message[0], message[1], part))

    def forward(h, message):
        i, j, part = message
        for direction, there in onward(message) if (i, j) != (0, 0) else ():
            n = INDEX[there]
            block = part_block(h, message, there[2])
            copy = remote(block, block, x_send.at[h, n], x_recv.at[h, n], way[direction])
            copy.start()
            sent.append(copy)
        n = OWN if (i, j) == (0, 0) else INDEX[message]
        block = block_of(c, h, message)
        copy = remote(block, block, d_send.at[h, n], d_recv.at[h, n], core_peer)
        copy.start()
        sent.append(copy)

    def take(h, message):
        n = INDEX[message]
        if n < 4:
            for piece, (first, count) in enumerate(PIECES):
                rows = pl.ds(pl.multiple_of(row_of(*message[:2]) + first, 16), count)
                block = wbuf.at[rows, half_cols]
                remote(block, block, o_send.at[piece, n], o_recv.at[piece, n], core_peer).wait_recv()
        else:
            block = block_of(c, h, message)
            remote(block, block, x_send.at[h, n], x_recv.at[h, n], core_peer).wait_recv()
        forward(h, message)

    def from_other_core(i, j):
        i_there, j_there = (-i if i % 2 else i), (-j if j % 2 else j)
        for h in range(H):
            for part in ("AB",) if 0 in (i, j) else ("A", "B"):
                n = OWN if (i, j) == (0, 0) else INDEX[(i_there, j_there, part)]
                block = block_of(1 - c, h, (i, j, part))
                remote(block, block, d_send.at[h, n], d_recv.at[h, n], core_peer).wait_recv()

    e = 2 * x_hi + c
    tile_row = lax.broadcasted_iota(jnp.int32, (8, 128), 0)

    def tile_of(row):
        low = jnp.broadcast_to(row[:, :128], (8, 128))
        high = jnp.broadcast_to(row[:, 128:], (8, 128))
        zero = jnp.zeros((8, 128), F32)
        return jnp.where(tile_row == e, low, jnp.where(tile_row == e + 4, high, zero))

    eown[...] = tile_of(emb)
    e_copies = []
    for k in range(1, 4):
        copy = remote(eown, erecv.at[k], e1_send.at[k], e1_recv.at[k], quad_peers[k - 1])
        copy.start()
        e_copies.append(copy)

    k_at = lax.broadcasted_iota(jnp.int32, (128, 128), 0)
    n_at = lax.broadcasted_iota(jnp.int32, (128, 128), 1)
    slot_at = n_at // 16
    away_at = jnp.where(slot_at % 2 == 1, (slot_at + 1) // 2, 8 - slot_at // 2)
    place[...] = jnp.where(k_at == (m + away_at) % 8 * 16 + n_at % 16, 1.0, 0.0).astype(BF16)

    for load in loads[1:]:
        load.wait()
    for n in range(16):
        cols = slice(128 * n, 128 * n + 128)
        valsp[:, cols] = jnp.dot(
            vals[:, cols], place[...], preferred_element_type=F32
        ).astype(BF16)

    for slot in (1, 2):
        z_wait(slot)
    own_piece(0)
    z_wait(3 + p)
    for k in (7, 6, 5):
        z_copy(k)

    for copy in g_copies:
        copy.wait_recv()
    limit = 8 * 192 - TXT + len_ref[0]

    def valid(width):
        return lax.broadcasted_iota(jnp.int32, (192, width), 0) + f * 192 < limit

    @pl.loop(0, 8)
    def _(n):
        cols = pl.ds(pl.multiple_of(n * 256, 256), 256)
        scaled = jnp.where(valid(256), cot[:, cols].astype(F32), 0.0)
        masked[:, cols] = (scaled * gate[0:1, cols]).astype(BF16)

    for slot in (4 - p, 5, 6, 7):
        z_wait(slot)
    own_piece(1)
    forward(0, (0, 0, "AB"))
    for i, j in AXIS:
        take(0, (i, j, "AB"))

    for copy in e_copies:
        copy.wait_recv()
    ebuf[z] = eown[...] + erecv[1] + erecv[2] + erecv[3]
    e2_copies = []
    for k in FAR_FIRST:
        copy = remote(ebuf.at[z], ebuf.at[z], e2_send.at[k], e2_recv.at[k], z_peers[k - 1])
        copy.start()
        e2_copies.append(copy)

    for i, j in AXIS:
        pass

    turned = (((1,), (1,)), ((), ()))
    probe_in = lax.dot_general(vals[...], inp[...], turned, preferred_element_type=F32).astype(BF16)
    probe_out = lax.dot_general(masked[...], outp[...], turned, preferred_element_type=F32).astype(BF16)
    projected = lax.dot_general(
        probe_in, probe_out, (((0,), (0,)), ((), ())), preferred_element_type=F32
    ) * (8 * 192) ** (-0.5)
    psend[...] = projected.reshape(8, 8, 64)
    p_copies = []
    for k in range(1, 8):
        copy = remote(psend.at[(f + k) % 8], precv.at[k], p_send.at[k], p_recv.at[k], f_peers[k - 1])
        copy.start()
        p_copies.append(copy)


    def pair_rows(i, j):
        xx, yy = (x + i + 8) % 2, (y + s * j + 8) % 4
        return pl.ds(pl.multiple_of(xx * 1024 + yy * 256, 256), 256)

    def branch(i, j, first=False):
        rows = pair_rows(i, j)

        product = jnp.dot(valsp[:, rows], wbuf[rows, :], preferred_element_type=F32)
        acc[...] = product if first else acc[...] + product

    def grad(i, j):
        rows = pair_rows(i, j)
        gradsp[:, rows] = lax.dot_general(
            masked[...], wbuf[rows, :], turned, preferred_element_type=F32
        ).astype(BF16)

    def pair_wait(i, j):
        for i_each in (0, 2) if i == 0 else (-1, 1):
            from_other_core(i_each, j)

    for message in FORWARDED:
        take(0, message)
    pair_wait(0, 0)
    branch(0, 0, first=True)
    pair_wait(1, 0)
    branch(1, 0)
    for message in SIDE:
        take(0, message)
    for j in (-1, 1):
        pair_wait(1, j)
        branch(1, j)
    grad(0, 0)
    grad(1, 0)
    for message in LAST:
        take(0, message)
    for i, j in ((0, -1), (0, 1), (1, 2), (0, 2)):
        pair_wait(i, j)
        branch(i, j)

    for n in range(8):
        cols = slice(256 * n, 256 * n + 256)
        scaled = jnp.where(valid(256), cot[:, cols].astype(F32), 0.0)
        tsend[n] = tile_of(jnp.sum(scaled * acc[:, cols], axis=0, keepdims=True))

    t1_copies = {}
    for n in sorted(range(1, 32), key=lambda n: -(n // 4 in (2, 6)) - (n % 4 in (1, 2, 3))):
        to_f, t = (f + n // 4) % 8, (e + n % 4) % 4
        copy = remote(
            tsend.at[to_f], trecv.at[n], t1_send.at[n], t1_recv.at[n],
            (to_f, (t // 2) * 32 + z * 2 + t % 2),
        )
        copy.start()
        t1_copies[n] = copy
    for n in range(8):
        cols = slice(256 * n, 256 * n + 256)
        mixed[:, cols] = (acc[:, cols] * gate[0:1, cols]).astype(BF16)
    store_mixed = pltpu.make_async_copy(mixed, mixed_out, l_sem.at[5])
    store_mixed.start()
    for i, j in ((1, -1), (1, 1), (0, -1)):
        grad(i, j)
    total = tsend[f]
    for n in range(1, 32):
        t1_copies[n].wait_recv()
        total = total + trecv[n]
    tbuf[z] = total
    t2_copies = []
    for k in FAR_FIRST:
        copy = remote(tbuf.at[z], tbuf.at[z], t2_send.at[k], t2_recv.at[k], z_peers[k - 1])
        copy.start()
        t2_copies.append(copy)
    for i, j in ((0, 1), (1, 2), (0, 2)):
        grad(i, j)
    for n in range(16):
        cols = slice(128 * n, 128 * n + 128)
        grads[:, cols] = lax.dot_general(
            gradsp[:, cols], place[...], turned, preferred_element_type=F32
        ).astype(BF16)
    store_grads = pltpu.make_async_copy(grads, grads_out, l_sem.at[6])
    store_grads.start()

    for copy in e2_copies:
        copy.wait_recv()
    emb_all = ebuf[...].reshape(128, 128) * (8 * 192 * 64) ** (-0.5)
    in_high = lax.broadcasted_iota(jnp.int32, (128, 128), 0) % 8 >= 4
    for half in range(2):
        for k_half in range(2):
            rows = emb_all
            if k_half != half:
                rows = pltpu.roll(emb_all, 4 if half else 124, 0)
            rows = jnp.where(in_high if half else jnp.logical_not(in_high), rows, 0.0)
            left[half, 128 * k_half : 128 * k_half + 128, :] = rows.T

    total = psend[f]
    for k in range(1, 8):
        p_copies[k - 1].wait_recv()
        total = total + precv[k]
    proj_out[...] = total
    for copy in q_copies + g_copies + sent + e_copies + e2_copies + p_copies + list(t1_copies.values()):
        copy.wait_send()
    for copy in t2_copies:
        copy.wait()
    grad_all = tbuf[...].reshape(128, 128)
    for half in range(2):
        gwg_out[:, 128 * half : 128 * half + 128] = jnp.dot(
            left[half], grad_all, precision=lax.Precision.HIGHEST, preferred_element_type=F32
        )
    store_mixed.wait()
    store_grads.wait()


def frequency_embedding(step_values, freq_width):
    half_width = freq_width // 2
    counter = jnp.arange(half_width, dtype=jnp.float32)
    frequencies = jnp.exp(-jnp.log(10000.0) * counter / half_width)
    angles = step_values.astype(jnp.float32)[:, None] * frequencies[None, :]
    return jnp.concatenate([jnp.cos(angles), jnp.sin(angles)], axis=-1)


def per_device(
    values, cotangent, out_weight, gate_weight, in_probe, out_probe, timesteps, text_lengths
):
    embedding = frequency_embedding(timesteps, 256)
    vmem = pl.BlockSpec(memory_space=pltpu.VMEM)
    smem = pl.BlockSpec(memory_space=pltpu.SMEM)
    anywhere = pl.BlockSpec(memory_space=pltpu.HBM)
    dma = pltpu.SemaphoreType.DMA
    count = OWN + 1
    mixed, grads, projected, gwg = pl.pallas_call(
        kernel,
        out_shape=(
            jax.ShapeDtypeStruct((192, 2048), BF16),
            jax.ShapeDtypeStruct((192, 2048), BF16),
            jax.ShapeDtypeStruct((8, 64), F32),
            jax.ShapeDtypeStruct((256, 256), F32),
        ),
        in_specs=[vmem, vmem, smem, anywhere, anywhere, anywhere, anywhere, anywhere],
        out_specs=(anywhere, anywhere, vmem, vmem),
        scratch_shapes=[
            pltpu.VMEM((2048, 2048), BF16),
            pltpu.VMEM((192, 2048), BF16),
            pltpu.VMEM((192, 2048), BF16),
            pltpu.VMEM((64, 2048), BF16),
            pltpu.VMEM((64, 2048), BF16),
            pltpu.VMEM((256, 256), BF16),
            pltpu.VMEM((192, 2048), BF16),
            pltpu.VMEM((128, 128), BF16),
            pltpu.VMEM((192, 2048), BF16),
            pltpu.VMEM((192, 2048), BF16),
            pltpu.VMEM((192, 2048), BF16),
            pltpu.VMEM((192, 2048), BF16),
            pltpu.VMEM((2, 256, 128), F32),
            pltpu.VMEM((192, 2048), F32),
            pltpu.VMEM((8, 2048), F32),
            pltpu.VMEM((4, 16, 512), BF16),
            pltpu.VMEM((8, 8, 64), F32),
            pltpu.VMEM((8, 8, 64), F32),
            pltpu.VMEM((8, 128), F32),
            pltpu.VMEM((4, 8, 128), F32),
            pltpu.VMEM((16, 8, 128), F32),
            pltpu.VMEM((8, 8, 128), F32),
            pltpu.VMEM((32, 8, 128), F32),
            pltpu.VMEM((16, 8, 128), F32),
            dma((7,)),
            dma((4,)), dma((4,)),
            dma((8,)), dma((8,)),
            dma((8,)), dma((8,)),
            dma((H, count)), dma((H, count)),
            dma((H, count)), dma((H, count)),
            dma((2, 4)), dma((2, 4)),
            dma((8,)), dma((8,)),
            dma((4,)), dma((4,)),
            dma((16,)), dma((16,)),
            dma((32,)), dma((32,)),
            dma((16,)), dma((16,)),
        ],
        compiler_params=pltpu.CompilerParams(
            collective_id=0, has_side_effects=True, vmem_limit_bytes=VMEM_BYTES
        ),
        cost_estimate=pl.CostEstimate(
            flops=4 * 192 * 2048 * 2048, bytes_accessed=8 * 192 * 2048, transcendentals=0
        ),
    )(
        out_weight, embedding, text_lengths, gate_weight,
        values[0], cotangent[0], in_probe.T, out_probe.T,
    )
    return mixed[None], grads[None], projected[None], gwg


def solution(mesh):
    in_specs = (
        P("dp", "fsdp", None),
        P("dp", "fsdp", None),
        P(("fsdp", "dp"), None),
        P(None, "fsdp"),
        P(),
        P(),
        P("dp"),
        P("dp"),
    )
    out_specs = (
        P("dp", "fsdp", None),
        P("dp", "fsdp", None),
        P("dp", "fsdp", None),
        P(None, "fsdp"),
    )
    return jax.shard_map(
        per_device, mesh=mesh, in_specs=in_specs, out_specs=out_specs, check_vma=False
    )
```

```python
import jax
import jax.numpy as jnp
from jax import lax
from jax.experimental import pallas as pl
from jax.experimental.pallas import tpu as pltpu
from jax.sharding import PartitionSpec as P

MESH = pl.DeviceIdType.MESH
F32, BF16 = jnp.float32, jnp.bfloat16
TXT = 256
GROUPS = ((0, 128),)
PIECES = ((0, 48), (48, 80))
H = len(GROUPS)
CHUNKS = 2
FAR_FIRST = (8, 7, 9, 6, 10, 5, 11, 4, 12, 3, 13, 2, 14, 1, 15)
VMEM_BYTES = 63 * 1024 * 1024

AXIS = [(-1, 0), (0, -1), (1, 0), (0, 1), (2, 0), (0, 2)]
FORWARDED = [(i, -1, "A") for i in (-1, 1, 2)] + [(-1, j, "B") for j in (-1, 1, 2)]
FORWARDED = [FORWARDED[n] for n in (0, 3, 1, 4, 2, 5)]
FINAL = [(i, j, "A") for j in (1, 2) for i in (-1, 1, 2)] + [
    (i, j, "B") for i in (1, 2) for j in (-1, 1, 2)
]
FINAL = [FINAL[n] for n in (0, 6, 1, 7, 2, 8, 3, 9, 4, 10, 5, 11)]
SIDE = [message for message in FINAL if message[:2] in ((-1, 1), (1, 1), (1, -1), (1, 2), (2, 1))]
SIDE = [message for message in SIDE if message not in ((1, 2, "A"), (2, 1, "B"))]
LAST = [message for message in FINAL if message not in SIDE]
MESSAGES = [(i, j, "AB") for i, j in AXIS] + FORWARDED + FINAL
INDEX = {message: n for n, message in enumerate(MESSAGES)}
OWN = len(MESSAGES)


def onward(message):
    i, j, part = message
    if part == "A":
        return [("yf", (i, 2, "A"))] if j == -1 else []
    if part == "B":
        return [("xf", (2, j, "B"))] if i == -1 else []
    if (i, j) == (0, 0):
        return [
            ("xf", (-1, 0, "AB")), ("yf", (0, -1, "AB")),
            ("xb", (1, 0, "AB")), ("yb", (0, 1, "AB")),
        ]
    if j == 0:
        first = [("xf", (2, 0, "AB"))] if i == -1 else []
        return first + [("yf", (i, -1, "A")), ("yb", (i, 1, "A"))]
    first = [("yf", (0, 2, "AB"))] if j == -1 else []
    return first + [("xf", (-1, j, "B")), ("xb", (1, j, "B"))]


def kernel(
    w_ref, step_ref, len_ref, gw_ref, values_ref, cot_ref, inp_ref, outp_ref,
    mixed_out, grads_out, proj_out, left, tbuf_out,
    wbuf, vals, cot, inp, outp, gw, valsp, place, masked, mixed, grads, gradsp, acc, gate,
    qbuf, psend, precv, eown, erecv, ebuf, tsend, trecv, tbuf,
    l_sem, q_send, q_recv, g_send, g_recv, z_send, z_recv, x_send, x_recv, d_send, d_recv, o_send, o_recv,
    p_send, p_recv, e1_send, e1_recv, e2_send, e2_recv, t1_send, t1_recv, t2_send, t2_recv,
):
    f, d = lax.axis_index("fsdp"), lax.axis_index("dp")
    x_lo, y = f // 4, f % 4
    x_hi, z, c = d // 32, (d // 2) % 16, d % 2
    x = 2 * x_hi + x_lo
    s = 1 - 2 * c
    m, p = z // 2, z % 2

    def device(xx, yy, zz, cc):
        return ((xx % 2) * 4 + yy, (xx // 2) * 32 + zz * 2 + cc)

    def remote(src, dst, send, recv, target):
        return pltpu.make_async_remote_copy(
            src_ref=src, dst_ref=dst, send_sem=send, recv_sem=recv,
            device_id=target, device_id_type=MESH,
        )

    loads = [
        pltpu.make_async_copy(a, b, l_sem.at[n])
        for n, (a, b) in enumerate(
            ((gw_ref, gw), (values_ref, vals), (cot_ref, cot), (inp_ref, inp), (outp_ref, outp))
        )
    ]
    for load in loads:
        load.start()

    here = (f, d)
    core_peer = device(x, y, z, 1 - c)
    z_peers = [device(x, y, (z + k) % 16, c) for k in range(1, 16)]
    f_peers = [((f + k) % 8, d) for k in range(1, 8)]
    quad_peers = []
    for k in range(1, 4):
        t = (2 * x_hi + c + k) % 4
        quad_peers.append((f, (t // 2) * 32 + z * 2 + t % 2))
    way = {
        "xf": device((x + s + 4) % 4, y, z, c),
        "xb": device((x - s + 4) % 4, y, z, c),
        "yf": device(x, (y + s + 4) % 4, z, c),
        "yb": device(x, (y - s + 4) % 4, z, c),
    }

    barrier = pltpu.get_barrier_semaphore()
    greeted = [z_peers[k - 1] for k in (4, 12, 3, 13, 2, 14, 1, 15)] + f_peers + quad_peers
    greeted = greeted + [
        (f, x_hi * 32 + (z + 1 - 2 * p) * 2 + 1 - c),
        ((1 - x_lo) * 4 + y, (1 - x_hi) * 32 + z * 2 + c),
    ]
    for peer in greeted:
        pl.semaphore_signal(barrier, inc=1, device_id=peer, device_id_type=MESH)

    mine = w_ref[...].astype(F32)
    t_own = 2 * p + c
    qbuf[t_own] = jnp.concatenate(
        [mine[:, 512 * n : 512 * n + 512] for n in range(4)], axis=0
    ).astype(BF16)
    pl.semaphore_wait(barrier, len(greeted))

    q_copies = []
    for k in range(1, 4):
        t = (t_own + k) % 4
        target = device(x, y, 2 * m + t // 2, t % 2)
        copy = remote(qbuf.at[t_own], qbuf.at[t_own], q_send.at[k], q_recv.at[k], target)
        copy.start()
        q_copies.append(copy)

    counter = lax.broadcasted_iota(jnp.int32, (1, 128), 1).astype(F32)
    angles = step_ref[0].astype(F32) * jnp.exp(-jnp.log(10000.0) * counter / 128)
    emb = jnp.concatenate([jnp.cos(angles), jnp.sin(angles)], axis=1)
    loads[0].wait()
    share = jnp.dot(
        jnp.broadcast_to(emb, (8, 256)), gw[...].astype(F32),
        precision=lax.Precision.HIGHEST, preferred_element_type=F32,
    )
    f_cols = pl.ds(pl.multiple_of(256 * f, 256), 256)
    gate[:, f_cols] = share
    g_copies = []
    for k in range(1, 8):
        copy = remote(gate.at[:, f_cols], gate.at[:, f_cols], g_send.at[k], g_recv.at[k], f_peers[k - 1])
        copy.start()
        g_copies.append(copy)

    for copy in q_copies:
        copy.wait_recv()
    quarter = [qbuf[t].astype(F32) for t in range(4)]
    low, high = [
        jnp.concatenate(
            [
                jnp.concatenate([quarter[t][4 * n : 4 * n + 4] for t in range(4)], axis=0)
                for n in pair
            ],
            axis=1,
        )
        for pair in ((0, 1), (2, 3))
    ]

    def row_of(i, j):
        xx, yy = (x + s * i + 8) % 4, (y + s * j + 8) % 4
        return (xx % 2) * 1024 + yy * 256 + (xx // 2) * 128

    def cols_of(core, part):
        start = 1024 * core + (512 if part == "B" else 0)
        return pl.ds(pl.multiple_of(start, 512), 1024 if part == "AB" else 512)

    own = row_of(0, 0)
    own_rows = pl.ds(pl.multiple_of(own, 16), 16)
    half_cols = cols_of(c, "AB")
    wbuf[own_rows, half_cols] = jnp.where(c == 0, low, high).astype(BF16)

    sent = []

    def z_rows(slot):
        return pl.ds(pl.multiple_of(own + 16 * slot, 16), 16)

    def z_copy(k):
        away = (k + 1) // 2
        slot = 2 * away - 1 + (p if away < 4 else 0)
        source, hops = (own_rows, k) if k <= 4 else (z_rows(3 + p), k - 4)
        copy = remote(
            wbuf.at[source, half_cols], wbuf.at[z_rows(slot), half_cols], z_send.at[k],
            z_recv.at[slot], device(x, y, (z + (2 * p - 1) * hops + 16) % 16, c),
        )
        copy.start()
        sent.append(copy)

    def z_wait(slot):
        block = wbuf.at[z_rows(slot), half_cols]
        remote(block, block, z_send.at[slot], z_recv.at[slot], core_peer).wait_recv()

    for k in (4, 1, 2, 3):
        z_copy(k)

    def block_of(core, h, message):
        i, j, part = message
        first, count = GROUPS[h]
        rows = pl.ds(pl.multiple_of(row_of(i, j) + first, 16), count)
        return wbuf.at[rows, cols_of(core, part)]


    def own_piece(piece):
        first, count = PIECES[piece]
        block = wbuf.at[pl.ds(pl.multiple_of(own + first, 16), count), half_cols]
        for direction, there in onward((0, 0, "AB")):
            n = INDEX[there]
            copy = remote(block, block, o_send.at[piece, n], o_recv.at[piece, n], way[direction])
            copy.start()
            sent.append(copy)

    def part_block(h, message, part):
        return block_of(c, h, (message[0], message[1], part))

    def forward(h, message):
        i, j, part = message
        for direction, there in onward(message) if (i, j) != (0, 0) else ():
            n = INDEX[there]
            block = part_block(h, message, there[2])
            copy = remote(block, block, x_send.at[h, n], x_recv.at[h, n], way[direction])
            copy.start()
            sent.append(copy)
        n = OWN if (i, j) == (0, 0) else INDEX[message]
        block = block_of(c, h, message)
        copy = remote(block, block, d_send.at[h, n], d_recv.at[h, n], core_peer)
        copy.start()
        sent.append(copy)

    def take(h, message):
        n = INDEX[message]
        if n < 4:
            for piece, (first, count) in enumerate(PIECES):
                rows = pl.ds(pl.multiple_of(row_of(*message[:2]) + first, 16), count)
                block = wbuf.at[rows, half_cols]
                remote(block, block, o_send.at[piece, n], o_recv.at[piece, n], core_peer).wait_recv()
        else:
            block = block_of(c, h, message)
            remote(block, block, x_send.at[h, n], x_recv.at[h, n], core_peer).wait_recv()
        forward(h, message)

    def from_other_core(i, j):
        i_there, j_there = (-i if i % 2 else i), (-j if j % 2 else j)
        for h in range(H):
            for part in ("AB",) if 0 in (i, j) else ("A", "B"):
                n = OWN if (i, j) == (0, 0) else INDEX[(i_there, j_there, part)]
                block = block_of(1 - c, h, (i, j, part))
                remote(block, block, d_send.at[h, n], d_recv.at[h, n], core_peer).wait_recv()

    e = 2 * x_hi + c
    tile_row = lax.broadcasted_iota(jnp.int32, (8, 128), 0)

    def tile_of(row):
        low = jnp.broadcast_to(row[:, :128], (8, 128))
        high = jnp.broadcast_to(row[:, 128:], (8, 128))
        zero = jnp.zeros((8, 128), F32)
        return jnp.where(tile_row == e, low, jnp.where(tile_row == e + 4, high, zero))

    eown[...] = tile_of(emb)
    e_copies = []
    for k in range(1, 4):
        copy = remote(eown, erecv.at[k], e1_send.at[k], e1_recv.at[k], quad_peers[k - 1])
        copy.start()
        e_copies.append(copy)

    k_at = lax.broadcasted_iota(jnp.int32, (128, 128), 0)
    n_at = lax.broadcasted_iota(jnp.int32, (128, 128), 1)
    slot_at = n_at // 16
    away_at = jnp.where(slot_at % 2 == 1, (slot_at + 1) // 2, 8 - slot_at // 2)
    place[...] = jnp.where(k_at == (m + away_at) % 8 * 16 + n_at % 16, 1.0, 0.0).astype(BF16)

    for load in loads[1:]:
        load.wait()
    for n in range(16):
        cols = slice(128 * n, 128 * n + 128)
        valsp[:, cols] = jnp.dot(
            vals[:, cols], place[...], preferred_element_type=F32
        ).astype(BF16)

    for slot in (1, 2):
        z_wait(slot)
    own_piece(0)
    z_wait(3 + p)
    for k in (7, 6, 5):
        z_copy(k)

    for copy in g_copies:
        copy.wait_recv()
    limit = 8 * 192 - TXT + len_ref[0]

    def valid(width):
        return lax.broadcasted_iota(jnp.int32, (192, width), 0) + f * 192 < limit

    @pl.loop(0, 8)
    def _(n):
        cols = pl.ds(pl.multiple_of(n * 256, 256), 256)
        scaled = jnp.where(valid(256), cot[:, cols].astype(F32), 0.0)
        masked[:, cols] = (scaled * gate[0:1, cols]).astype(BF16)

    for slot in (4 - p, 5, 6, 7):
        z_wait(slot)
    own_piece(1)
    forward(0, (0, 0, "AB"))
    for i, j in AXIS:
        take(0, (i, j, "AB"))

    for copy in e_copies:
        copy.wait_recv()
    ebuf[z] = eown[...] + erecv[1] + erecv[2] + erecv[3]
    e2_copies = []
    for k in FAR_FIRST:
        copy = remote(ebuf.at[z], ebuf.at[z], e2_send.at[k], e2_recv.at[k], z_peers[k - 1])
        copy.start()
        e2_copies.append(copy)

    for i, j in AXIS:
        pass

    turned = (((1,), (1,)), ((), ()))
    probe_in = lax.dot_general(vals[...], inp[...], turned, preferred_element_type=F32).astype(BF16)
    probe_out = lax.dot_general(masked[...], outp[...], turned, preferred_element_type=F32).astype(BF16)
    projected = lax.dot_general(
        probe_in, probe_out, (((0,), (0,)), ((), ())), preferred_element_type=F32
    ) * (8 * 192) ** (-0.5)
    psend[...] = projected.reshape(8, 8, 64)
    p_copies = []
    for k in range(1, 8):
        copy = remote(psend.at[(f + k) % 8], precv.at[k], p_send.at[k], p_recv.at[k], f_peers[k - 1])
        copy.start()
        p_copies.append(copy)


    def pair_rows(i, j):
        xx, yy = (x + i + 8) % 2, (y + s * j + 8) % 4
        return pl.ds(pl.multiple_of(xx * 1024 + yy * 256, 256), 256)

    def branch(i, j, first=False):
        rows = pair_rows(i, j)

        product = jnp.dot(valsp[:, rows], wbuf[rows, :], preferred_element_type=F32)
        acc[...] = product if first else acc[...] + product

    def grad(i, j):
        rows = pair_rows(i, j)
        gradsp[:, rows] = lax.dot_general(
            masked[...], wbuf[rows, :], turned, preferred_element_type=F32
        ).astype(BF16)

    def pair_wait(i, j):
        for i_each in (0, 2) if i == 0 else (-1, 1):
            from_other_core(i_each, j)

    for message in FORWARDED:
        take(0, message)
    pair_wait(0, 0)
    branch(0, 0, first=True)
    pair_wait(1, 0)
    branch(1, 0)
    for message in SIDE:
        take(0, message)
    for j in (-1, 1):
        pair_wait(1, j)
        branch(1, j)
    grad(0, 0)
    grad(1, 0)
    for message in LAST:
        take(0, message)
    for i, j in ((0, -1), (0, 1), (1, 2), (0, 2)):
        pair_wait(i, j)
        branch(i, j)

    for n in range(8):
        cols = slice(256 * n, 256 * n + 256)
        scaled = jnp.where(valid(256), cot[:, cols].astype(F32), 0.0)
        tsend[n] = tile_of(jnp.sum(scaled * acc[:, cols], axis=0, keepdims=True))

    t1_copies = {}
    for n in sorted(range(1, 32), key=lambda n: -(n // 4 in (2, 6)) - (n % 4 in (1, 2, 3))):
        to_f, t = (f + n // 4) % 8, (e + n % 4) % 4
        copy = remote(
            tsend.at[to_f], trecv.at[n], t1_send.at[n], t1_recv.at[n],
            (to_f, (t // 2) * 32 + z * 2 + t % 2),
        )
        copy.start()
        t1_copies[n] = copy
    for n in range(8):
        cols = slice(256 * n, 256 * n + 256)
        mixed[:, cols] = (acc[:, cols] * gate[0:1, cols]).astype(BF16)
    store_mixed = pltpu.make_async_copy(mixed, mixed_out, l_sem.at[5])
    store_mixed.start()
    for i, j in ((1, -1), (1, 1), (0, -1)):
        grad(i, j)
    total = tsend[f]
    for n in range(1, 32):
        t1_copies[n].wait_recv()
        total = total + trecv[n]
    tbuf[z] = total
    t2_copies = []
    for k in FAR_FIRST:
        copy = remote(tbuf.at[z], tbuf.at[z], t2_send.at[k], t2_recv.at[k], z_peers[k - 1])
        copy.start()
        t2_copies.append(copy)
    for i, j in ((0, 1), (1, 2), (0, 2)):
        grad(i, j)
    for n in range(16):
        cols = slice(128 * n, 128 * n + 128)
        grads[:, cols] = lax.dot_general(
            gradsp[:, cols], place[...], turned, preferred_element_type=F32
        ).astype(BF16)
    store_grads = pltpu.make_async_copy(grads, grads_out, l_sem.at[6])
    store_grads.start()

    for copy in e2_copies:
        copy.wait_recv()
    emb_all = ebuf[...].reshape(128, 128) * (8 * 192 * 64) ** (-0.5)
    in_high = lax.broadcasted_iota(jnp.int32, (128, 128), 0) % 8 >= 4
    for half in range(2):
        for k_half in range(2):
            rows = emb_all
            if k_half != half:
                rows = pltpu.roll(emb_all, 4 if half else 124, 0)
            rows = jnp.where(in_high if half else jnp.logical_not(in_high), rows, 0.0)
            left[half, 128 * k_half : 128 * k_half + 128, :] = rows.T

    total = psend[f]
    for k in range(1, 8):
        p_copies[k - 1].wait_recv()
        total = total + precv[k]
    proj_out[...] = total
    for copy in q_copies + g_copies + sent + e_copies + e2_copies + p_copies + list(t1_copies.values()):
        copy.wait_send()
    for copy in t2_copies:
        copy.wait()
    tbuf_out[...] = tbuf[...]
    store_mixed.wait()
    store_grads.wait()


def finish(
    mixed, grads, proj, left, gathered, mixed_out, grads_out, proj_out, gwg_out,
    mixed_buf, grads_buf, proj_buf, left_buf, gathered_buf, gwg_buf, in_sem, out_sem,
):
    small = [
        pltpu.make_async_copy(left, left_buf, in_sem.at[0]),
        pltpu.make_async_copy(gathered, gathered_buf, in_sem.at[1]),
    ]
    through = [(proj, proj_buf, proj_out)]
    for n in range(CHUNKS):
        rows = pl.ds(n * (192 // CHUNKS), 192 // CHUNKS)
        through.append((mixed.at[rows], mixed_buf.at[rows], mixed_out.at[rows]))
        through.append((grads.at[rows], grads_buf.at[rows], grads_out.at[rows]))
    fetches = [
        pltpu.make_async_copy(a, b, in_sem.at[2 + n]) for n, (a, b, _) in enumerate(through)
    ]
    stores = [
        pltpu.make_async_copy(b, o, out_sem.at[1 + n]) for n, (_, b, o) in enumerate(through)
    ]
    for copy in small + fetches:
        copy.start()
    for copy in small:
        copy.wait()
    grad_all = gathered_buf[...].reshape(128, 128)
    for half in range(2):
        gwg_buf[:, 128 * half : 128 * half + 128] = jnp.dot(
            left_buf[half], grad_all, precision=lax.Precision.HIGHEST, preferred_element_type=F32
        )
    gwg_store = pltpu.make_async_copy(gwg_buf, gwg_out, out_sem.at[0])
    gwg_store.start()
    for fetch, store in zip(fetches, stores):
        fetch.wait()
        store.start()
    for copy in stores + [gwg_store]:
        copy.wait()


def per_device(
    values, cotangent, out_weight, gate_weight, in_probe, out_probe, timesteps, text_lengths
):
    vmem = pl.BlockSpec(memory_space=pltpu.VMEM)
    smem = pl.BlockSpec(memory_space=pltpu.SMEM)
    anywhere = pl.BlockSpec(memory_space=pltpu.HBM)
    dma = pltpu.SemaphoreType.DMA
    count = OWN + 1
    mixed, grads, projected, left, gathered = pl.pallas_call(
        kernel,
        out_shape=(
            jax.ShapeDtypeStruct((192, 2048), BF16),
            jax.ShapeDtypeStruct((192, 2048), BF16),
            jax.ShapeDtypeStruct((8, 64), F32),
            jax.ShapeDtypeStruct((2, 256, 128), F32),
            jax.ShapeDtypeStruct((16, 8, 128), F32),
        ),
        in_specs=[vmem, smem, smem, anywhere, anywhere, anywhere, anywhere, anywhere],
        out_specs=(anywhere, anywhere, vmem, vmem, vmem),
        scratch_shapes=[
            pltpu.VMEM((2048, 2048), BF16),
            pltpu.VMEM((192, 2048), BF16),
            pltpu.VMEM((192, 2048), BF16),
            pltpu.VMEM((64, 2048), BF16),
            pltpu.VMEM((64, 2048), BF16),
            pltpu.VMEM((256, 256), BF16),
            pltpu.VMEM((192, 2048), BF16),
            pltpu.VMEM((128, 128), BF16),
            pltpu.VMEM((192, 2048), BF16),
            pltpu.VMEM((192, 2048), BF16),
            pltpu.VMEM((192, 2048), BF16),
            pltpu.VMEM((192, 2048), BF16),
            pltpu.VMEM((192, 2048), F32),
            pltpu.VMEM((8, 2048), F32),
            pltpu.VMEM((4, 16, 512), BF16),
            pltpu.VMEM((8, 8, 64), F32),
            pltpu.VMEM((8, 8, 64), F32),
            pltpu.VMEM((8, 128), F32),
            pltpu.VMEM((4, 8, 128), F32),
            pltpu.VMEM((16, 8, 128), F32),
            pltpu.VMEM((8, 8, 128), F32),
            pltpu.VMEM((32, 8, 128), F32),
            pltpu.VMEM((16, 8, 128), F32),
            dma((7,)),
            dma((4,)), dma((4,)),
            dma((8,)), dma((8,)),
            dma((8,)), dma((8,)),
            dma((H, count)), dma((H, count)),
            dma((H, count)), dma((H, count)),
            dma((2, 4)), dma((2, 4)),
            dma((8,)), dma((8,)),
            dma((4,)), dma((4,)),
            dma((16,)), dma((16,)),
            dma((32,)), dma((32,)),
            dma((16,)), dma((16,)),
        ],
        compiler_params=pltpu.CompilerParams(
            collective_id=0, has_side_effects=True, vmem_limit_bytes=VMEM_BYTES
        ),
        cost_estimate=pl.CostEstimate(
            flops=4 * 192 * 2048 * 2048, bytes_accessed=8 * 192 * 2048, transcendentals=0
        ),
    )(
        out_weight, timesteps, text_lengths, gate_weight,
        values[0], cotangent[0], in_probe.T, out_probe.T,
    )
    mixed, grads, projected, gwg = pl.pallas_call(
        finish,
        out_shape=(
            jax.ShapeDtypeStruct((192, 2048), BF16),
            jax.ShapeDtypeStruct((192, 2048), BF16),
            jax.ShapeDtypeStruct((8, 64), F32),
            jax.ShapeDtypeStruct((256, 256), F32),
        ),
        in_specs=[anywhere] * 5,
        out_specs=(anywhere, anywhere, anywhere, anywhere),
        scratch_shapes=[
            pltpu.VMEM((192, 2048), BF16),
            pltpu.VMEM((192, 2048), BF16),
            pltpu.VMEM((8, 64), F32),
            pltpu.VMEM((2, 256, 128), F32),
            pltpu.VMEM((16, 8, 128), F32),
            pltpu.VMEM((256, 256), F32),
            dma((3 + 2 * CHUNKS,)),
            dma((2 + 2 * CHUNKS,)),
        ],
        compiler_params=pltpu.CompilerParams(vmem_limit_bytes=VMEM_BYTES),
    )(mixed, grads, projected, left, gathered)
    return mixed[None], grads[None], projected[None], gwg


def solution(mesh):
    in_specs = (
        P("dp", "fsdp", None),
        P("dp", "fsdp", None),
        P(("fsdp", "dp"), None),
        P(None, "fsdp"),
        P(),
        P(),
        P("dp"),
        P("dp"),
    )
    out_specs = (
        P("dp", "fsdp", None),
        P("dp", "fsdp", None),
        P("dp", "fsdp", None),
        P(None, "fsdp"),
    )
    return jax.shard_map(
        per_device, mesh=mesh, in_specs=in_specs, out_specs=out_specs, check_vma=False
    )
```

```python
import jax
import jax.numpy as jnp
from jax import lax
from jax.experimental import pallas as pl
from jax.experimental.pallas import tpu as pltpu
from jax.sharding import PartitionSpec as P

MESH = pl.DeviceIdType.MESH
F32, BF16 = jnp.float32, jnp.bfloat16
TXT = 256
GROUPS = ((0, 128),)
PIECES = ((0, 48), (48, 80))
H = len(GROUPS)
CHUNKS = 2
FAR_FIRST = (8, 7, 9, 6, 10, 5, 11, 4, 12, 3, 13, 2, 14, 1, 15)
VMEM_BYTES = 63 * 1024 * 1024

AXIS = [(-1, 0), (0, -1), (1, 0), (0, 1), (2, 0), (0, 2)]
FORWARDED = [(i, -1, "A") for i in (-1, 1, 2)] + [(-1, j, "B") for j in (-1, 1, 2)]
FORWARDED = [FORWARDED[n] for n in (0, 3, 1, 4, 2, 5)]
FINAL = [(i, j, "A") for j in (1, 2) for i in (-1, 1, 2)] + [
    (i, j, "B") for i in (1, 2) for j in (-1, 1, 2)
]
FINAL = [FINAL[n] for n in (0, 6, 1, 7, 2, 8, 3, 9, 4, 10, 5, 11)]
SIDE = [message for message in FINAL if message[:2] in ((-1, 1), (1, 1), (1, -1), (1, 2), (2, 1))]
SIDE = [message for message in SIDE if message not in ((1, 2, "A"), (2, 1, "B"))]
LAST = [message for message in FINAL if message not in SIDE]
MESSAGES = [(i, j, "AB") for i, j in AXIS] + FORWARDED + FINAL
INDEX = {message: n for n, message in enumerate(MESSAGES)}
OWN = len(MESSAGES)


def onward(message):
    i, j, part = message
    if part == "A":
        return [("yf", (i, 2, "A"))] if j == -1 else []
    if part == "B":
        return [("xf", (2, j, "B"))] if i == -1 else []
    if (i, j) == (0, 0):
        return [
            ("xf", (-1, 0, "AB")), ("yf", (0, -1, "AB")),
            ("xb", (1, 0, "AB")), ("yb", (0, 1, "AB")),
        ]
    if j == 0:
        first = [("xf", (2, 0, "AB"))] if i == -1 else []
        return first + [("yf", (i, -1, "A")), ("yb", (i, 1, "A"))]
    first = [("yf", (0, 2, "AB"))] if j == -1 else []
    return first + [("xf", (-1, j, "B")), ("xb", (1, j, "B"))]


def kernel(
    w_ref, step_ref, len_ref, gw_ref, values_ref, cot_ref, inp_ref, outp_ref,
    mixed_out, grads_out, proj_out, left, tbuf_out,
    wbuf, vals, cot, inp, outp, gw, valsp, place, masked, mixed, grads, gradsp, acc, gate,
    qbuf, psend, precv, eown, erecv, ebuf, tsend, trecv, tbuf,
    l_sem, q_send, q_recv, g_send, g_recv, z_send, z_recv, x_send, x_recv, d_send, d_recv, o_send, o_recv,
    p_send, p_recv, e1_send, e1_recv, e2_send, e2_recv, t1_send, t1_recv, t2_send, t2_recv,
):
    f, d = lax.axis_index("fsdp"), lax.axis_index("dp")
    x_lo, y = f // 4, f % 4
    x_hi, z, c = d // 32, (d // 2) % 16, d % 2
    x = 2 * x_hi + x_lo
    s = 1 - 2 * c
    m, p = z // 2, z % 2

    def device(xx, yy, zz, cc):
        return ((xx % 2) * 4 + yy, (xx // 2) * 32 + zz * 2 + cc)

    def remote(src, dst, send, recv, target):
        return pltpu.make_async_remote_copy(
            src_ref=src, dst_ref=dst, send_sem=send, recv_sem=recv,
            device_id=target, device_id_type=MESH,
        )

    loads = [
        pltpu.make_async_copy(a, b, l_sem.at[n])
        for n, (a, b) in enumerate(
            ((gw_ref, gw), (values_ref, vals), (cot_ref, cot), (inp_ref, inp), (outp_ref, outp))
        )
    ]
    for load in loads:
        load.start()

    here = (f, d)
    core_peer = device(x, y, z, 1 - c)
    z_peers = [device(x, y, (z + k) % 16, c) for k in range(1, 16)]
    f_peers = [((f + k) % 8, d) for k in range(1, 8)]
    quad_peers = []
    for k in range(1, 4):
        t = (2 * x_hi + c + k) % 4
        quad_peers.append((f, (t // 2) * 32 + z * 2 + t % 2))
    way = {
        "xf": device((x + s + 4) % 4, y, z, c),
        "xb": device((x - s + 4) % 4, y, z, c),
        "yf": device(x, (y + s + 4) % 4, z, c),
        "yb": device(x, (y - s + 4) % 4, z, c),
    }

    barrier = pltpu.get_barrier_semaphore()
    greeted = [z_peers[k - 1] for k in (4, 12, 3, 13, 2, 14, 1, 15)] + f_peers + quad_peers
    greeted = greeted + [
        (f, x_hi * 32 + (z + 1 - 2 * p) * 2 + 1 - c),
        ((1 - x_lo) * 4 + y, (1 - x_hi) * 32 + z * 2 + c),
    ]
    for peer in greeted:
        pl.semaphore_signal(barrier, inc=1, device_id=peer, device_id_type=MESH)

    mine = w_ref[...].astype(F32)
    t_own = 2 * p + c
    qbuf[t_own] = jnp.concatenate(
        [mine[:, 512 * n : 512 * n + 512] for n in range(4)], axis=0
    ).astype(BF16)
    pl.semaphore_wait(barrier, len(greeted))

    q_copies = []
    for k in range(1, 4):
        t = (t_own + k) % 4
        target = device(x, y, 2 * m + t // 2, t % 2)
        copy = remote(qbuf.at[t_own], qbuf.at[t_own], q_send.at[k], q_recv.at[k], target)
        copy.start()
        q_copies.append(copy)

    counter = lax.broadcasted_iota(jnp.int32, (1, 128), 1).astype(F32)
    angles = step_ref[0].astype(F32) * jnp.exp(-jnp.log(10000.0) * counter / 128)
    emb = jnp.concatenate([jnp.cos(angles), jnp.sin(angles)], axis=1)
    loads[0].wait()
    share = jnp.dot(
        jnp.broadcast_to(emb, (8, 256)), gw[...].astype(F32),
        precision=lax.Precision.HIGHEST, preferred_element_type=F32,
    )
    f_cols = pl.ds(pl.multiple_of(256 * f, 256), 256)
    gate[:, f_cols] = share
    g_copies = []
    for k in range(1, 8):
        copy = remote(gate.at[:, f_cols], gate.at[:, f_cols], g_send.at[k], g_recv.at[k], f_peers[k - 1])
        copy.start()
        g_copies.append(copy)

    for copy in q_copies:
        copy.wait_recv()
    quarter = [qbuf[t].astype(F32) for t in range(4)]
    low, high = [
        jnp.concatenate(
            [
                jnp.concatenate([quarter[t][4 * n : 4 * n + 4] for t in range(4)], axis=0)
                for n in pair
            ],
            axis=1,
        )
        for pair in ((0, 1), (2, 3))
    ]

    def row_of(i, j):
        xx, yy = (x + s * i + 8) % 4, (y + s * j + 8) % 4
        return (xx % 2) * 1024 + yy * 256 + (xx // 2) * 128

    def cols_of(core, part):
        start = 1024 * core + (512 if part == "B" else 0)
        return pl.ds(pl.multiple_of(start, 512), 1024 if part == "AB" else 512)

    own = row_of(0, 0)
    own_rows = pl.ds(pl.multiple_of(own, 16), 16)
    half_cols = cols_of(c, "AB")
    wbuf[own_rows, half_cols] = jnp.where(c == 0, low, high).astype(BF16)

    sent = []

    def z_rows(slot):
        return pl.ds(pl.multiple_of(own + 16 * slot, 16), 16)

    def z_copy(k):
        away = (k + 1) // 2
        slot = 2 * away - 1 + (p if away < 4 else 0)
        source, hops = (own_rows, k) if k <= 4 else (z_rows(3 + p), k - 4)
        copy = remote(
            wbuf.at[source, half_cols], wbuf.at[z_rows(slot), half_cols], z_send.at[k],
            z_recv.at[slot], device(x, y, (z + (2 * p - 1) * hops + 16) % 16, c),
        )
        copy.start()
        sent.append(copy)

    def z_wait(slot):
        block = wbuf.at[z_rows(slot), half_cols]
        remote(block, block, z_send.at[slot], z_recv.at[slot], core_peer).wait_recv()

    for k in (4, 1, 2, 3):
        z_copy(k)

    def block_of(core, h, message):
        i, j, part = message
        first, count = GROUPS[h]
        rows = pl.ds(pl.multiple_of(row_of(i, j) + first, 16), count)
        return wbuf.at[rows, cols_of(core, part)]


    def own_piece(piece):
        first, count = PIECES[piece]
        block = wbuf.at[pl.ds(pl.multiple_of(own + first, 16), count), half_cols]
        for direction, there in onward((0, 0, "AB")):
            n = INDEX[there]
            copy = remote(block, block, o_send.at[piece, n], o_recv.at[piece, n], way[direction])
            copy.start()
            sent.append(copy)

    def part_block(h, message, part):
        return block_of(c, h, (message[0], message[1], part))

    def forward(h, message):
        i, j, part = message
        for direction, there in onward(message) if (i, j) != (0, 0) else ():
            n = INDEX[there]
            block = part_block(h, message, there[2])
            copy = remote(block, block, x_send.at[h, n], x_recv.at[h, n], way[direction])
            copy.start()
            sent.append(copy)
        n = OWN if (i, j) == (0, 0) else INDEX[message]
        block = block_of(c, h, message)
        copy = remote(block, block, d_send.at[h, n], d_recv.at[h, n], core_peer)
        copy.start()
        sent.append(copy)

    def take(h, message):
        n = INDEX[message]
        if n < 4:
            for piece, (first, count) in enumerate(PIECES):
                rows = pl.ds(pl.multiple_of(row_of(*message[:2]) + first, 16), count)
                block = wbuf.at[rows, half_cols]
                remote(block, block, o_send.at[piece, n], o_recv.at[piece, n], core_peer).wait_recv()
        else:
            block = block_of(c, h, message)
            remote(block, block, x_send.at[h, n], x_recv.at[h, n], core_peer).wait_recv()
        forward(h, message)

    def from_other_core(i, j):
        i_there, j_there = (-i if i % 2 else i), (-j if j % 2 else j)
        for h in range(H):
            for part in ("AB",) if 0 in (i, j) else ("A", "B"):
                n = OWN if (i, j) == (0, 0) else INDEX[(i_there, j_there, part)]
                block = block_of(1 - c, h, (i, j, part))
                remote(block, block, d_send.at[h, n], d_recv.at[h, n], core_peer).wait_recv()

    e = 2 * x_hi + c
    tile_row = lax.broadcasted_iota(jnp.int32, (8, 128), 0)

    def tile_of(row):
        low = jnp.broadcast_to(row[:, :128], (8, 128))
        high = jnp.broadcast_to(row[:, 128:], (8, 128))
        zero = jnp.zeros((8, 128), F32)
        return jnp.where(tile_row == e, low, jnp.where(tile_row == e + 4, high, zero))

    eown[...] = tile_of(emb)
    e_copies = []
    for k in range(1, 4):
        copy = remote(eown, erecv.at[k], e1_send.at[k], e1_recv.at[k], quad_peers[k - 1])
        copy.start()
        e_copies.append(copy)

    k_at = lax.broadcasted_iota(jnp.int32, (128, 128), 0)
    n_at = lax.broadcasted_iota(jnp.int32, (128, 128), 1)
    slot_at = n_at // 16
    away_at = jnp.where(slot_at % 2 == 1, (slot_at + 1) // 2, 8 - slot_at // 2)
    place[...] = jnp.where(k_at == (m + away_at) % 8 * 16 + n_at % 16, 1.0, 0.0).astype(BF16)

    for load in loads[1:]:
        load.wait()
    for n in range(16):
        cols = slice(128 * n, 128 * n + 128)
        valsp[:, cols] = jnp.dot(
            vals[:, cols], place[...], preferred_element_type=F32
        ).astype(BF16)

    for slot in (1, 2):
        z_wait(slot)
    own_piece(0)
    z_wait(3 + p)
    for k in (7, 6, 5):
        z_copy(k)

    for copy in g_copies:
        copy.wait_recv()
    limit = 8 * 192 - TXT + len_ref[0]

    def valid(width):
        return lax.broadcasted_iota(jnp.int32, (192, width), 0) + f * 192 < limit

    @pl.loop(0, 8)
    def _(n):
        cols = pl.ds(pl.multiple_of(n * 256, 256), 256)
        scaled = jnp.where(valid(256), cot[:, cols].astype(F32), 0.0)
        masked[:, cols] = (scaled * gate[0:1, cols]).astype(BF16)

    for slot in (4 - p, 5, 6, 7):
        z_wait(slot)
    own_piece(1)
    forward(0, (0, 0, "AB"))
    for i, j in AXIS:
        take(0, (i, j, "AB"))

    for copy in e_copies:
        copy.wait_recv()
    ebuf[z] = eown[...] + erecv[1] + erecv[2] + erecv[3]
    e2_copies = []
    for k in FAR_FIRST:
        copy = remote(ebuf.at[z], ebuf.at[z], e2_send.at[k], e2_recv.at[k], z_peers[k - 1])
        copy.start()
        e2_copies.append(copy)

    for i, j in AXIS:
        pass

    turned = (((1,), (1,)), ((), ()))
    probe_in = lax.dot_general(vals[...], inp[...], turned, preferred_element_type=F32).astype(BF16)
    probe_out = lax.dot_general(masked[...], outp[...], turned, preferred_element_type=F32).astype(BF16)
    projected = lax.dot_general(
        probe_in, probe_out, (((0,), (0,)), ((), ())), preferred_element_type=F32
    ) * (8 * 192) ** (-0.5)
    psend[...] = projected.reshape(8, 8, 64)
    p_copies = []
    for k in range(1, 8):
        copy = remote(psend.at[(f + k) % 8], precv.at[k], p_send.at[k], p_recv.at[k], f_peers[k - 1])
        copy.start()
        p_copies.append(copy)


    def pair_rows(i, j):
        xx, yy = (x + i + 8) % 2, (y + s * j + 8) % 4
        return pl.ds(pl.multiple_of(xx * 1024 + yy * 256, 256), 256)

    def branch(i, j, first=False):
        rows = pair_rows(i, j)

        product = jnp.dot(valsp[:, rows], wbuf[rows, :], preferred_element_type=F32)
        acc[...] = product if first else acc[...] + product

    def grad(i, j):
        rows = pair_rows(i, j)
        gradsp[:, rows] = lax.dot_general(
            masked[...], wbuf[rows, :], turned, preferred_element_type=F32
        ).astype(BF16)

    def pair_wait(i, j):
        for i_each in (0, 2) if i == 0 else (-1, 1):
            from_other_core(i_each, j)

    for message in FORWARDED:
        take(0, message)
    pair_wait(0, 0)
    branch(0, 0, first=True)
    pair_wait(1, 0)
    branch(1, 0)
    for message in SIDE:
        take(0, message)
    for j in (-1, 1):
        pair_wait(1, j)
        branch(1, j)
    grad(0, 0)
    grad(1, 0)
    for message in LAST:
        take(0, message)
    for i, j in ((0, -1), (0, 1), (1, 2), (0, 2)):
        pair_wait(i, j)
        branch(i, j)

    for n in range(8):
        cols = slice(256 * n, 256 * n + 256)
        scaled = jnp.where(valid(256), cot[:, cols].astype(F32), 0.0)
        tsend[n] = tile_of(jnp.sum(scaled * acc[:, cols], axis=0, keepdims=True))

    t1_copies = {}
    for n in sorted(range(1, 32), key=lambda n: -(n // 4 in (2, 6)) - (n % 4 in (1, 2, 3))):
        to_f, t = (f + n // 4) % 8, (e + n % 4) % 4
        copy = remote(
            tsend.at[to_f], trecv.at[n], t1_send.at[n], t1_recv.at[n],
            (to_f, (t // 2) * 32 + z * 2 + t % 2),
        )
        copy.start()
        t1_copies[n] = copy
    for n in range(8):
        cols = slice(256 * n, 256 * n + 256)
        mixed[:, cols] = (acc[:, cols] * gate[0:1, cols]).astype(BF16)
    store_mixed = pltpu.make_async_copy(mixed, mixed_out, l_sem.at[5])
    store_mixed.start()
    for i, j in ((1, -1), (1, 1), (0, -1)):
        grad(i, j)
    total = tsend[f]
    for n in range(1, 32):
        t1_copies[n].wait_recv()
        total = total + trecv[n]
    tbuf[z] = total
    t2_copies = []
    for k in FAR_FIRST:
        copy = remote(tbuf.at[z], tbuf.at[z], t2_send.at[k], t2_recv.at[k], z_peers[k - 1])
        copy.start()
        t2_copies.append(copy)
    for i, j in ((0, 1), (1, 2), (0, 2)):
        grad(i, j)
    for n in range(16):
        cols = slice(128 * n, 128 * n + 128)
        grads[:, cols] = lax.dot_general(
            gradsp[:, cols], place[...], turned, preferred_element_type=F32
        ).astype(BF16)
    store_grads = pltpu.make_async_copy(grads, grads_out, l_sem.at[6])
    store_grads.start()

    for copy in e2_copies:
        copy.wait_recv()
    emb_all = ebuf[...].reshape(128, 128) * (8 * 192 * 64) ** (-0.5)
    in_high = lax.broadcasted_iota(jnp.int32, (128, 128), 0) % 8 >= 4
    for half in range(2):
        for k_half in range(2):
            rows = emb_all
            if k_half != half:
                rows = pltpu.roll(emb_all, 4 if half else 124, 0)
            rows = jnp.where(in_high if half else jnp.logical_not(in_high), rows, 0.0)
            left[half, 128 * k_half : 128 * k_half + 128, :] = rows.T

    total = psend[f]
    for k in range(1, 8):
        p_copies[k - 1].wait_recv()
        total = total + precv[k]
    proj_out[...] = total
    for copy in q_copies + g_copies + sent + e_copies + e2_copies + p_copies + list(t1_copies.values()):
        copy.wait_send()
    for copy in t2_copies:
        copy.wait()
    tbuf_out[...] = tbuf[...]
    store_mixed.wait()
    store_grads.wait()


def finish(
    mixed, grads, proj, left, gathered, mixed_out, grads_out, proj_out, gwg_out,
    mixed_buf, grads_buf, proj_buf, left_buf, gathered_buf, gwg_buf, in_sem, out_sem,
):
    small = [
        pltpu.make_async_copy(left, left_buf, in_sem.at[0]),
        pltpu.make_async_copy(gathered, gathered_buf, in_sem.at[1]),
    ]
    through = [(proj, proj_buf, proj_out)]
    for n in range(CHUNKS):
        rows = pl.ds(n * (192 // CHUNKS), 192 // CHUNKS)
        through.append((mixed.at[rows], mixed_buf.at[rows], mixed_out.at[rows]))
        through.append((grads.at[rows], grads_buf.at[rows], grads_out.at[rows]))
    fetches = [
        pltpu.make_async_copy(a, b, in_sem.at[2 + n]) for n, (a, b, _) in enumerate(through)
    ]
    stores = [
        pltpu.make_async_copy(b, o, out_sem.at[1 + n]) for n, (_, b, o) in enumerate(through)
    ]
    for copy in small + fetches:
        copy.start()
    for fetch, store in zip(fetches, stores):
        fetch.wait()
        store.start()
    for copy in small:
        copy.wait()
    grad_all = gathered_buf[...].reshape(128, 128)
    for half in range(2):
        gwg_buf[:, 128 * half : 128 * half + 128] = jnp.dot(
            left_buf[half], grad_all, precision=lax.Precision.HIGHEST, preferred_element_type=F32
        )
    gwg_store = pltpu.make_async_copy(gwg_buf, gwg_out, out_sem.at[0])
    gwg_store.start()
    for copy in stores + [gwg_store]:
        copy.wait()


def per_device(
    values, cotangent, out_weight, gate_weight, in_probe, out_probe, timesteps, text_lengths
):
    vmem = pl.BlockSpec(memory_space=pltpu.VMEM)
    smem = pl.BlockSpec(memory_space=pltpu.SMEM)
    anywhere = pl.BlockSpec(memory_space=pltpu.HBM)
    dma = pltpu.SemaphoreType.DMA
    count = OWN + 1
    mixed, grads, projected, left, gathered = pl.pallas_call(
        kernel,
        out_shape=(
            jax.ShapeDtypeStruct((192, 2048), BF16),
            jax.ShapeDtypeStruct((192, 2048), BF16),
            jax.ShapeDtypeStruct((8, 64), F32),
            jax.ShapeDtypeStruct((2, 256, 128), F32),
            jax.ShapeDtypeStruct((16, 8, 128), F32),
        ),
        in_specs=[vmem, smem, smem, anywhere, anywhere, anywhere, anywhere, anywhere],
        out_specs=(anywhere, anywhere, vmem, vmem, vmem),
        scratch_shapes=[
            pltpu.VMEM((2048, 2048), BF16),
            pltpu.VMEM((192, 2048), BF16),
            pltpu.VMEM((192, 2048), BF16),
            pltpu.VMEM((64, 2048), BF16),
            pltpu.VMEM((64, 2048), BF16),
            pltpu.VMEM((256, 256), BF16),
            pltpu.VMEM((192, 2048), BF16),
            pltpu.VMEM((128, 128), BF16),
            pltpu.VMEM((192, 2048), BF16),
            pltpu.VMEM((192, 2048), BF16),
            pltpu.VMEM((192, 2048), BF16),
            pltpu.VMEM((192, 2048), BF16),
            pltpu.VMEM((192, 2048), F32),
            pltpu.VMEM((8, 2048), F32),
            pltpu.VMEM((4, 16, 512), BF16),
            pltpu.VMEM((8, 8, 64), F32),
            pltpu.VMEM((8, 8, 64), F32),
            pltpu.VMEM((8, 128), F32),
            pltpu.VMEM((4, 8, 128), F32),
            pltpu.VMEM((16, 8, 128), F32),
            pltpu.VMEM((8, 8, 128), F32),
            pltpu.VMEM((32, 8, 128), F32),
            pltpu.VMEM((16, 8, 128), F32),
            dma((7,)),
            dma((4,)), dma((4,)),
            dma((8,)), dma((8,)),
            dma((8,)), dma((8,)),
            dma((H, count)), dma((H, count)),
            dma((H, count)), dma((H, count)),
            dma((2, 4)), dma((2, 4)),
            dma((8,)), dma((8,)),
            dma((4,)), dma((4,)),
            dma((16,)), dma((16,)),
            dma((32,)), dma((32,)),
            dma((16,)), dma((16,)),
        ],
        compiler_params=pltpu.CompilerParams(
            collective_id=0, has_side_effects=True, vmem_limit_bytes=VMEM_BYTES
        ),
        cost_estimate=pl.CostEstimate(
            flops=4 * 192 * 2048 * 2048, bytes_accessed=8 * 192 * 2048, transcendentals=0
        ),
    )(
        out_weight, timesteps, text_lengths, gate_weight,
        values[0], cotangent[0], in_probe.T, out_probe.T,
    )
    mixed, grads, projected, gwg = pl.pallas_call(
        finish,
        out_shape=(
            jax.ShapeDtypeStruct((192, 2048), BF16),
            jax.ShapeDtypeStruct((192, 2048), BF16),
            jax.ShapeDtypeStruct((8, 64), F32),
            jax.ShapeDtypeStruct((256, 256), F32),
        ),
        in_specs=[anywhere] * 5,
        out_specs=(anywhere, anywhere, anywhere, anywhere),
        scratch_shapes=[
            pltpu.VMEM((192, 2048), BF16),
            pltpu.VMEM((192, 2048), BF16),
            pltpu.VMEM((8, 64), F32),
            pltpu.VMEM((2, 256, 128), F32),
            pltpu.VMEM((16, 8, 128), F32),
            pltpu.VMEM((256, 256), F32),
            dma((3 + 2 * CHUNKS,)),
            dma((2 + 2 * CHUNKS,)),
        ],
        compiler_params=pltpu.CompilerParams(vmem_limit_bytes=VMEM_BYTES),
    )(mixed, grads, projected, left, gathered)
    return mixed[None], grads[None], projected[None], gwg


def solution(mesh):
    in_specs = (
        P("dp", "fsdp", None),
        P("dp", "fsdp", None),
        P(("fsdp", "dp"), None),
        P(None, "fsdp"),
        P(),
        P(),
        P("dp"),
        P("dp"),
    )
    out_specs = (
        P("dp", "fsdp", None),
        P("dp", "fsdp", None),
        P("dp", "fsdp", None),
        P(None, "fsdp"),
    )
    return jax.shard_map(
        per_device, mesh=mesh, in_specs=in_specs, out_specs=out_specs, check_vma=False
    )
```
